128 devices in a mesh: gx: 8 (over x_lo, y), gy: 16 (over x_hi, z, core).
Axes of the slice: x: 4 (x_hi: 2, x_lo: 2; x = x_hi * 2 + x_lo), y: 4, z: 4, core: 2. Of those that a mesh axis runs over, the one named last changes fastest.
Arguments:
- velocity: float32 [80, 160, 64], P('gy', None, 'gx'), may hold values from 1.5 to 4.5
- forward_now: float32 [320, 640, 256], P('gx', 'gy'), may hold values from -6 to 6
- forward_before: float32 [320, 640, 256], P('gx', 'gy'), may hold values from -6 to 6
- adjoint_now: float32 [320, 640, 256], P('gx', 'gy'), may hold values from -6 to 6
- adjoint_after: float32 [320, 640, 256], P('gx', 'gy'), may hold values from -6 to 6
- source_cells: int32 [3, 4], replicated, may hold values from 0 to 639, as said below
- receiver_cells: int32 [3, 1024], replicated, may hold values from 0 to 639, as said below
- wavelet: float32 [4, 4], replicated, may hold values from -24 to 24
- observed: float32 [4, 1024], replicated, may hold values from -24 to 24
Outputs:
- gradient: float32 [80, 160, 64], P('gy', None, 'gx')
The draws below stay inside these ranges and needn't reach their ends.
Inputs may be any that keep to these rules, and one draw needn't show every extreme that they name: `source_cells`: row 0 holds x cells of 0 to 319, row 1 y cells of 0 to 639, row 2 z cells of 0 to 255; the first source sits at the cell (319, 639, 255) and the second at (0, 0, 0); cells may repeat. `receiver_cells`: row 0 holds x cells of 0 to 319, row 1 y cells of 0 to 639, row 2 z cells of 0 to 255; the first receiver sits at the cell (319, 639, 255) and the second at (0, 0, 0); cells may repeat.
All inputs are finite; a program needn't handle non-finite values.
Results may differ from the reference program's by a relative error of at most 0.0003.
Values sent between devices are 32-bit elements; how exact they have to be, the bound alone decides.
No kernel may reach another device: no remote copies, remote signals or barrier semaphores. Data moves between devices by JAX's collectives and lax.ppermute only.
A program may use at most 128 MiB of HBM per device.

```python
import jax
import jax.numpy as jnp
from jax import lax

NZ = 256
ITERS = 4
NSRC = 4
NREC = 1024
NX = 320
NY = 640
MX = 80
MY = 160
MZ = 64


def place_cells(key, number):
    sub_keys = jax.random.split(key, 3)
    along_x = jax.random.randint(sub_keys[0], (number,), 0, NX, dtype=jnp.int32)
    along_y = jax.random.randint(sub_keys[1], (number,), 0, NY, dtype=jnp.int32)
    along_z = jax.random.randint(sub_keys[2], (number,), 0, NZ, dtype=jnp.int32)
    along_x = along_x.at[0].set(NX - 1).at[1].set(0)
    along_y = along_y.at[0].set(NY - 1).at[1].set(0)
    along_z = along_z.at[0].set(NZ - 1).at[1].set(0)
    return jnp.stack([along_x, along_y, along_z]).astype(jnp.int32)


def draw_source_cells(key, part):
    key = jax.random.fold_in(key, 5)
    return place_cells(key, NSRC)


def draw_receiver_cells(key, part):
    key = jax.random.fold_in(key, 9)
    return place_cells(key, NREC)


def shard_levels(key, extent, pieces, least, high):
    factor_of, own = 1.0, jax.random.fold_in(key, 6)
    for dim, blocks in pieces:
        draws = jnp.exp(jax.random.uniform(jax.random.fold_in(own, dim), (blocks,), jnp.float32, least / len(pieces), high / len(pieces)))
        factor_of = factor_of * jnp.repeat(draws, extent[dim] // blocks).reshape([-1 if axis == dim else 1 for axis in range(len(extent))])
    return factor_of


def noise(rng, dims, deviation, limit, cuts=(), kind=jnp.bfloat16):
    result = jax.random.normal(rng, dims, jnp.float32) * deviation
    if len(cuts) > 0:
        result = shard_levels(rng, dims, cuts, -0.22, 0.18) * result
    return jnp.clip(result, min=-limit, max=limit).astype(kind)


def setup_inputs(seed: int = 0) -> dict:
    key_of = jax.random.split(jax.random.key(seed), 10)
    return {
        "velocity": jnp.clip(1.5 + 3.0 * jax.random.uniform(key_of[0], (MX, MY, MZ), jnp.float32) ** shard_levels(key_of[0], (MX, MY, MZ), ((0, 16), (2, 8)), -0.2, 0.2), 1.5, 4.5),
        "forward_now": noise(key_of[1], (NX, NY, NZ), 1.0, 6.0, ((0, 8), (1, 16)), jnp.float32),
        "forward_before": noise(key_of[2], (NX, NY, NZ), 1.0, 6.0, ((0, 8), (1, 16)), jnp.float32),
        "adjoint_now": noise(key_of[3], (NX, NY, NZ), 1.0, 6.0, ((0, 8), (1, 16)), jnp.float32),
        "adjoint_after": noise(key_of[4], (NX, NY, NZ), 1.0, 6.0, ((0, 8), (1, 16)), jnp.float32),
        "source_cells": draw_source_cells(jax.random.fold_in(key_of[9], 71), 0),
        "receiver_cells": draw_receiver_cells(jax.random.fold_in(key_of[9], 71), 0),
        "wavelet": noise(key_of[7], (ITERS, NSRC), 4.0, 24.0, (), jnp.float32),
        "observed": noise(key_of[8], (ITERS, NREC), 4.0, 24.0, (), jnp.float32),
    }


COEFFS = (-205.0 / 72.0, 8.0 / 5.0, -1.0 / 5.0, 8.0 / 315.0, -1.0 / 560.0)


def weights(fine_count, coarse):
    position = jnp.arange(fine_count, dtype=jnp.int32)
    lower = position // 4
    higher = jnp.minimum(lower + 1, coarse - 1)
    fraction = (position % 4).astype(jnp.float32) * 0.25
    column = jnp.arange(coarse, dtype=jnp.int32)
    first = jnp.where(column[None, :] == lower[:, None], 1.0 - fraction[:, None], 0.0)
    second = jnp.where(column[None, :] == higher[:, None], fraction[:, None], 0.0)
    return (first + second).astype(jnp.float32)


def laplacian(padded):
    span_x = padded.shape[0] - 8
    span_y = padded.shape[1] - 8
    span_z = padded.shape[2] - 8

    def shifted(move_x, move_y, move_z):
        return padded[4 + move_x:4 + move_x + span_x, 4 + move_y:4 + move_y + span_y, 4 + move_z:4 + move_z + span_z]

    result_sum = 3.0 * COEFFS[0] * shifted(0, 0, 0)
    for reach in range(1, 5):
        pairs = shifted(reach, 0, 0) + shifted(-reach, 0, 0) + shifted(0, reach, 0) + shifted(0, -reach, 0)
        pairs = pairs + shifted(0, 0, reach) + shifted(0, 0, -reach)
        result_sum = result_sum + COEFFS[reach] * pairs
    return result_sum


def reference(velocity, forward_now, forward_before, adjoint_now, adjoint_after, source_cells, receiver_cells, wavelet, observed):
    coarse_x, coarse_y, coarse_z = velocity.shape
    cells_x, cells_y, cells_z = forward_now.shape
    exact = lax.Precision.HIGHEST
    weight_x = weights(cells_x, coarse_x)
    weight_y = weights(cells_y, coarse_y)
    weight_z = weights(cells_z, coarse_z)
    fine_speed = jnp.einsum('abc,zc->abz', velocity, weight_z, precision=exact)
    fine_speed = jnp.einsum('abz,yb->ayz', fine_speed, weight_y, precision=exact)
    fine_speed = jnp.einsum('ayz,xa->xyz', fine_speed, weight_x, precision=exact)
    courant = fine_speed * fine_speed * 0.01
    source_flat = ((source_cells[0] * cells_y + source_cells[1]) * cells_z + source_cells[2]).astype(jnp.int32)
    receiver_flat = ((receiver_cells[0] * cells_y + receiver_cells[1]) * cells_z + receiver_cells[2]).astype(jnp.int32)
    before, field_now = forward_before, forward_now
    accel_list = []
    residual_list = []
    for section in range(ITERS):
        accel = courant * laplacian(jnp.pad(field_now, 4))
        accel = accel.reshape(-1).at[source_flat].add(wavelet[section]).reshape(field_now.shape)
        field_after = 2.0 * field_now - before + accel
        residual_list.append(field_after.reshape(-1)[receiver_flat] - observed[section])
        accel_list.append(accel)
        before, field_now = field_now, field_after
    field_later, field_now = adjoint_after, adjoint_now
    image_sum = jnp.zeros_like(field_now)
    for section in reversed(range(ITERS)):
        change = laplacian(jnp.pad(courant * field_now, 4))
        change = change.reshape(-1).at[receiver_flat].add(residual_list[section]).reshape(field_now.shape)
        earlier = 2.0 * field_now - field_later + change
        image_sum = image_sum + earlier * accel_list[section]
        field_later, field_now = field_now, earlier
    image_sum = image_sum * 2.0 / fine_speed
    coarse_part = jnp.einsum('xyz,xa->ayz', image_sum, weight_x, precision=exact)
    coarse_part = jnp.einsum('ayz,yb->abz', coarse_part, weight_y, precision=exact)
    coarse_part = jnp.einsum('abz,zc->abc', coarse_part, weight_z, precision=exact)
    return coarse_part * 0.125
```

```python
import jax
import jax.numpy as jnp
from jax import lax
from jax.experimental import pallas as pl
from jax.experimental.pallas import tpu as pltpu
from jax.sharding import PartitionSpec as P

ITERS = 4
HALO = 16
OWN = 40
EXT = OWN + 2 * HALO
LANES = 128
ACC_ROWS = 48
ACC_PLANES = 44
CENTRE = -43050.0
RING = (8064.0, -1008.0, 128.0, -9.0)
SCALE = 5040.0
SMEM = pltpu.SMEM
VMEM = pltpu.VMEM
EXACT = lax.Precision.HIGHEST


def params(mib):
    return pltpu.CompilerParams(vmem_limit_bytes=mib * 1024 * 1024)


def z_matrix():
    row = lax.broadcasted_iota(jnp.int32, (512, 256), 0) & 255
    column = lax.broadcasted_iota(jnp.int32, (512, 256), 1)
    distance = jnp.abs(row - column)
    result = jnp.zeros((512, 256), jnp.float32)
    for reach, value in enumerate(RING):
        result = jnp.where(distance == reach + 1, value, result)
    return result.astype(jnp.bfloat16)


def hat(fine, coarse, lower, limit, fraction):
    higher = jnp.minimum(lower + 1, limit)
    first = jnp.where(coarse == lower, 1.0 - fraction, 0.0)
    second = jnp.where(coarse == higher, fraction, 0.0)
    return first + second


def list_kernel(base_ref, cells_ref, own_ref, ext_ref, count_ref):
    base_x = base_ref[0] - (HALO - 4)
    base_y = base_ref[1] - (HALO - 4)
    span = EXT - 8

    def body(receiver, carry):
        own, ext = carry
        x = cells_ref[receiver] - base_x
        y = cells_ref[1024 + receiver] - base_y
        z = cells_ref[2048 + receiver]
        packed = receiver | (z << 10) | (y << 18) | (x << 25)
        in_ext = (x >= 0) & (x < span) & (y >= 0) & (y < span)
        in_own = (x >= 12) & (x < 52) & (y >= 12) & (y < 52)
        own_ref[own] = packed
        ext_ref[ext] = packed
        return own + in_own.astype(jnp.int32), ext + in_ext.astype(jnp.int32)

    own, ext = lax.fori_loop(0, 1024, body, (0, 0), unroll=8)
    count_ref[0] = own
    count_ref[1] = ext


def unpack(packed):
    receiver = packed & 1023
    z = (packed >> 10) & 255
    y = (packed >> 18) & 127
    x = packed >> 25
    return receiver, x + 4, y + 4, z


def model_kernel(base_ref, model_ref, courant_ref, inverse_ref, plane_ref):
    row = lax.broadcasted_iota(jnp.int32, (64, 256), 0)
    column = lax.broadcasted_iota(jnp.int32, (64, 256), 1)
    weight_z = hat(column, row, column // 4, 63, (column & 3).astype(jnp.float32) * 0.25)
    deep = jnp.dot(
        model_ref[...].reshape(480, 64), weight_z, precision=EXACT,
        preferred_element_type=jnp.float32,
    ).reshape(20, 24, 256)
    fine = lax.broadcasted_iota(jnp.int32, (EXT, 24), 0)
    coarse = lax.broadcasted_iota(jnp.int32, (EXT, 24), 1)
    limit_y = 159 - (base_ref[1] // 4 - 3)
    weight_y = hat(fine, coarse, fine // 4 - 1, limit_y, (fine & 3).astype(jnp.float32) * 0.25)
    place = fine + (base_ref[1] - HALO)
    weight_y = jnp.where((place >= 0) & (place < 640), weight_y, 0.0)
    for a in range(2, 19):
        plane = jnp.dot(weight_y, deep[a], precision=EXACT, preferred_element_type=jnp.float32)
        plane_ref[a, 0] = plane[:, :LANES]
        plane_ref[a, 1] = plane[:, LANES:]
    limit_x = 79 - (base_ref[0] // 4 - 5)
    factor = 0.01 / SCALE

    def group(index, carry):
        a = index + 1
        higher = jnp.minimum(a + 1, limit_x)
        start = base_ref[0] - HALO + 4 * index
        inside = ((start >= 0) & (start < 320)).astype(jnp.float32) * factor
        for half in range(2):
            for tile in range(EXT // 8):
                rows = pl.ds(8 * tile, 8)
                low = plane_ref[a, half, rows, :]
                high = plane_ref[higher, half, rows, :]
                for step in range(4):
                    speed = low * (1.0 - 0.25 * step) + high * (0.25 * step)
                    courant_ref[4 * index + step, half, rows, :] = speed * speed * inside
        return carry

    lax.fori_loop(1, 17, group, 0)

    def invert(index, carry):
        a = index + 5
        higher = jnp.minimum(a + 1, limit_x)
        for half in range(2):
            for tile in range(OWN // 8):
                rows = pl.ds(HALO + 8 * tile, 8)
                low = plane_ref[a, half, rows, :]
                high = plane_ref[higher, half, rows, :]
                for step in range(4):
                    speed = low * (1.0 - 0.25 * step) + high * (0.25 * step)
                    inverse_ref[4 * index + step, half, pl.ds(8 * tile, 8), :] = 2.0 / speed
        return carry

    lax.fori_loop(0, 10, invert, 0)


def copies(now, before, pieces, ext_now, ext_before):
    x_low, x_high, y_low, y_high, c_low, c_high = pieces
    result = []
    mid = pl.ds(HALO, OWN)
    for half in range(2):
        lanes = pl.ds(half * LANES, LANES)

        def add(source, planes, rows, target, to_planes, to_rows):
            result.append(
                (source.at[planes, rows, lanes], target.at[to_planes, half, to_rows, :])
            )

        every = pl.ds(0, OWN)
        add(now, every, every, ext_now, mid, mid)
        add(x_low, pl.ds(0, 16), every, ext_now, pl.ds(0, 16), mid)
        add(x_high, pl.ds(0, 16), every, ext_now, pl.ds(56, 16), mid)
        add(y_low, every, pl.ds(0, 16), ext_now, mid, pl.ds(0, 16))
        add(y_high, every, pl.ds(0, 16), ext_now, mid, pl.ds(56, 16))
        add(before, every, every, ext_before, mid, mid)
        add(x_low, pl.ds(16, 12), every, ext_before, pl.ds(4, 12), mid)
        add(x_high, pl.ds(16, 12), every, ext_before, pl.ds(56, 12), mid)
        add(y_low, pl.ds(40, 40), pl.ds(0, 16), ext_before, mid, pl.ds(0, 16))
        add(y_high, pl.ds(40, 40), pl.ds(0, 16), ext_before, mid, pl.ds(56, 16))
        for piece, near, far in ((c_low, 8, 0), (c_high, 56, 64)):
            for side, first in ((0, 12), (24, 56)):
                rows = pl.ds(0, 8)
                second = 4 if side == 0 else 60
                third = 8 if side == 0 else 56
                add(piece, pl.ds(side, 4), rows, ext_now, pl.ds(first, 4), pl.ds(far, 8))
                add(piece, pl.ds(side + 4, 4), rows, ext_now, pl.ds(first, 4), pl.ds(near, 8))
                add(piece, pl.ds(side + 8, 8), rows, ext_now, pl.ds(second, 8), pl.ds(near, 8))
                add(piece, pl.ds(side + 16, 8), rows, ext_before, pl.ds(third, 8), pl.ds(near, 8))
    return result


def start_all(pairs, sem):
    started = [pltpu.make_async_copy(a, b, sem) for a, b in pairs]
    for copy in started:
        copy.start()
    return started


def wait_all(started):
    for copy in started:
        copy.wait()


def stencil_pass(source, matrix_ref, step, emit):
    first = 4 * step
    span = EXT - 8 * step
    tiles = span // 8

    def group(index, carry):
        x = first + 4 * index
        whole = [
            source[pl.ds(x, 4), half, pl.ds(first, span), :].reshape(4 * span, LANES)
            for half in range(2)
        ]
        whole = jnp.concatenate(whole, axis=1)
        upper = whole.astype(jnp.bfloat16)
        lower = (whole - upper.astype(jnp.float32)).astype(jnp.bfloat16)
        along_z = jnp.dot(
            jnp.concatenate([upper, lower], axis=1), matrix_ref[...],
            preferred_element_type=jnp.float32,
        )
        for tile in range(tiles):
            for half in range(2):
                row = first + 8 * tile
                window = [source[x - 4 + j, half, pl.ds(row, 8), :] for j in range(12)]
                for g in range(4):
                    start = g * span + 8 * tile
                    total = along_z[start : start + 8, half * LANES : (half + 1) * LANES]
                    total = total + CENTRE * window[4 + g]
                    for reach in range(1, 5):
                        pair_x = window[4 + g + reach] + window[4 + g - reach]
                        pair_y = (
                            source[x + g, half, pl.ds(row + reach, 8), :]
                            + source[x + g, half, pl.ds(row - reach, 8), :]
                        )
                        total = total + RING[reach - 1] * (pair_x + pair_y)
                    emit(x, g, half, row, window[4 + g], total)
        return carry

    lax.fori_loop(0, span // 4, group, 0)


def own_plane(x, g):
    inside = (x >= HALO) & (x < HALO + OWN)
    return jnp.where(inside, x - HALO, OWN) + g


def forward_kernel(
    base_ref, source_ref, wavelet_ref, own_ref, count_ref, receivers_ref, observed_ref, matrix_ref,
    now, before, x_low, x_high, y_low, y_high, c_low, c_high, courant_in,
    accel_out, residual_ref,
    field_a, field_b, field_c, field_d, courant, accel, sems,
):
    loads = start_all(
        copies(now, before, (x_low, x_high, y_low, y_high, c_low, c_high), field_b, field_a)
        + [(courant_in, courant)],
        sems.at[0],
    )
    wait_all(loads)
    lane = lax.broadcasted_iota(jnp.int32, (1, LANES), 1)
    fields = [field_a, field_b, field_a, field_b, field_c, field_d]
    stores = []
    for step in range(1, ITERS + 1):
        older, newer, target = fields[step - 1], fields[step], fields[step + 1]

        def emit(x, g, half, row, centre, total):
            rows = pl.ds(row, 8)
            change = courant[x + g, half, rows, :] * total
            if HALO - 8 < row < HALO + OWN:
                accel[step - 1, own_plane(x, g), half, pl.ds(row - 12, 8), :] = change
            target[x + g, half, rows, :] = (
                centre + centre - older[x + g, half, rows, :] + change
            )

        if step == ITERS:
            def emit(x, g, half, row, centre, total):
                rows = pl.ds(row, 8)
                change = courant[x + g, half, rows, :] * total
                accel[step - 1, x + g - HALO, half, pl.ds(row - 12, 8), :] = change
                target[x + g, half, rows, :] = (
                    centre + centre - older[x + g, half, rows, :] + change
                )

        stencil_pass(newer, matrix_ref, step, emit)
        for source in range(4):
            x = source_ref[source] - (base_ref[0] - HALO)
            y = source_ref[4 + source] - (base_ref[1] - HALO)
            z = source_ref[8 + source]
            amount = wavelet_ref[4 * (step - 1) + source]

            @pl.when((x >= 0) & (x < EXT) & (y >= 0) & (y < EXT))
            def _():
                half = z // LANES
                added = jnp.where(lane == (z & (LANES - 1)), amount, 0.0)
                target[x, half, pl.ds(y, 1), :] += added

                @pl.when((x >= 16) & (x < 56) & (y >= 16) & (y < 56))
                def _():
                    accel[step - 1, x - 16, half, pl.ds(y - 12, 1), :] += added

        stores += start_all([(accel.at[step - 1], accel_out.at[step - 1])], sems.at[1])
    number = count_ref[0]
    place = (
        lax.broadcasted_iota(jnp.int32, (8, LANES), 0) * LANES
        + lax.broadcasted_iota(jnp.int32, (8, LANES), 1)
    )
    samples = fields[2:]

    def sample(index, carry):
        carry = list(carry)
        for j in range(4):
            entry = 4 * index + j
            valid = entry < number
            packed = jnp.where(valid, own_ref[jnp.minimum(entry, 1023)], 0)
            receiver, x, y, z = unpack(packed)
            half = z // LANES
            at_lane = lane == jnp.where(valid, z & (LANES - 1), -1)
            at_place = place == jnp.where(valid, receiver, -1)
            for step in range(ITERS):
                values = jnp.where(at_lane, samples[step][x, half, pl.ds(y, 1), :], 0.0)
                value = jnp.sum(values, axis=1, keepdims=True)
                carry[step] = jnp.where(at_place, value, carry[step])
        return tuple(carry)

    zero = jnp.zeros((8, LANES), jnp.float32)
    sampled = lax.fori_loop(0, (number + 3) // 4, sample, (zero,) * ITERS)
    local_x = receivers_ref[0] - base_ref[0]
    local_y = receivers_ref[1] - base_ref[1]
    mine = (local_x >= 0) & (local_x < OWN) & (local_y >= 0) & (local_y < OWN)
    for step in range(ITERS):
        residual_ref[step] = jnp.where(mine, sampled[step] - observed_ref[step], 0.0)
    wait_all(stores)


def adjoint_kernel(
    base_ref, ext_ref, count_ref, residual_ref, matrix_ref,
    now, after, x_low, x_high, y_low, y_high, c_low, c_high, courant_in, accel_in, inverse_in,
    out_ref,
    field_a, field_b, field_c, field_d, scaled_a, scaled_b, courant, accel, inverse, coarse, sems,
):
    loads = start_all(
        copies(now, after, (x_low, x_high, y_low, y_high, c_low, c_high), field_b, field_a)
        + [(courant_in, courant)],
        sems.at[0],
    )
    later = start_all([(accel_in, accel), (inverse_in, inverse)], sems.at[1])
    wait_all(loads)

    def scale(x, carry):
        for half in range(2):
            for tile in range(EXT // 8):
                rows = pl.ds(8 * tile, 8)
                scaled_a[x, half, rows, :] = field_b[x, half, rows, :] * courant[x, half, rows, :]
        return carry

    lax.fori_loop(0, EXT, scale, 0)
    lane = lax.broadcasted_iota(jnp.int32, (1, LANES), 1)
    fields = [field_a, field_b, field_a, field_b, field_c, field_d]
    number = count_ref[1]
    for step in range(1, ITERS + 1):
        older, newer, target = fields[step - 1], fields[step], fields[step + 1]
        source, scaled = (scaled_a, scaled_b) if step % 2 else (scaled_b, scaled_a)

        def emit(x, g, half, row, centre, total):
            rows = pl.ds(row, 8)
            middle = newer[x + g, half, rows, :]
            value = middle + middle - older[x + g, half, rows, :] + total
            target[x + g, half, rows, :] = value
            if step < ITERS:
                scaled[x + g, half, rows, :] = value * courant[x + g, half, rows, :]

        stencil_pass(source, matrix_ref, step, emit)

        def inject(entry, carry):
            receiver, x, y, z = unpack(ext_ref[entry])
            half = z // LANES
            amount = residual_ref[(ITERS - step) * 1024 + receiver]
            added = jnp.where(lane == (z & (LANES - 1)), amount, 0.0)
            target[x, half, pl.ds(y, 1), :] += added
            if step < ITERS:
                scaled[x, half, pl.ds(y, 1), :] += added * courant[x, half, pl.ds(y, 1), :]
            return carry

        lax.fori_loop(0, number, inject, 0)
    wait_all(later)
    coarse[...] = jnp.zeros(coarse.shape, jnp.float32)
    limit_x = 79 - base_ref[0] // 4

    def image(a, carry):
        higher = jnp.minimum(a + 1, limit_x)
        for half in range(2):
            for tile in range(OWN // 8):
                rows = pl.ds(8 * tile, 8)
                low, high = None, None
                for g in range(4):
                    x = 4 * a + g
                    total = None
                    for step in range(1, ITERS + 1):
                        term = (
                            fields[step + 1][x + HALO, half, pl.ds(HALO + 8 * tile, 8), :]
                            * accel[ITERS - step, x, half, pl.ds(4 + 8 * tile, 8), :]
                        )
                        total = term if total is None else total + term
                    total = total * inverse[x, half, rows, :]
                    weight = 0.25 * g
                    low = total if low is None else low + (1.0 - weight) * total
                    if g:
                        part = weight * total
                        high = part if high is None else high + part
                coarse[a, half, rows, :] += low
                coarse[higher, half, rows, :] += high
        return carry

    lax.fori_loop(0, 10, image, 0)
    row = lax.broadcasted_iota(jnp.int32, (16, OWN), 0)
    fine = lax.broadcasted_iota(jnp.int32, (16, OWN), 1)
    limit_y = 159 - base_ref[1] // 4
    weight_y = hat(fine, row, fine // 4, limit_y, (fine & 3).astype(jnp.float32) * 0.25)
    fine = lax.broadcasted_iota(jnp.int32, (256, 64), 0)
    column = lax.broadcasted_iota(jnp.int32, (256, 64), 1)
    weight_z = hat(fine, column, fine // 4, 63, (fine & 3).astype(jnp.float32) * 0.25)
    parts = []
    for a in range(11):
        plane = jnp.concatenate([coarse[a, 0], coarse[a, 1]], axis=1)
        parts.append(
            jnp.dot(weight_y, plane, precision=EXACT, preferred_element_type=jnp.float32)
        )
    stacked = jnp.concatenate(parts, axis=0)
    result = jnp.dot(stacked, weight_z, precision=EXACT, preferred_element_type=jnp.float32)
    out_ref[...] = (result * 0.125).reshape(11, 16, 64)


def shifts(axis, block_up, block_down):
    count = lax.axis_size(axis)
    up = [(i, i + 1) for i in range(count - 1)]
    down = [(i + 1, i) for i in range(count - 1)]
    return lax.ppermute(block_up, axis, up), lax.ppermute(block_down, axis, down)


def exchange_x(now, before):
    return shifts(
        "gx",
        jnp.concatenate([now[24:], before[28:]], axis=0),
        jnp.concatenate([now[:16], before[:12]], axis=0),
    )


def exchange_y(now, before):
    return shifts(
        "gy",
        jnp.concatenate([now[:, 24:], before[:, 24:]], axis=0),
        jnp.concatenate([now[:, :16], before[:, :16]], axis=0),
    )


def exchange_corners(x_low, x_high):
    up = [
        x_low[12:16, 24:32], x_low[12:16, 32:40], x_low[4:12, 32:40], x_low[20:28, 32:40],
        x_high[0:4, 24:32], x_high[0:4, 32:40], x_high[4:12, 32:40], x_high[16:24, 32:40],
    ]
    down = [
        x_low[12:16, 8:16], x_low[12:16, 0:8], x_low[4:12, 0:8], x_low[20:28, 0:8],
        x_high[0:4, 8:16], x_high[0:4, 0:8], x_high[4:12, 0:8], x_high[16:24, 0:8],
    ]
    return shifts("gy", jnp.concatenate(up, axis=0), jnp.concatenate(down, axis=0))


def exchange(now, before):
    x_low, x_high = exchange_x(now, before)
    y_low, y_high = exchange_y(now, before)
    c_low, c_high = exchange_corners(x_low, x_high)
    return (x_low, x_high, y_low, y_high, c_low, c_high)


def spec(space):
    return pl.BlockSpec(memory_space=space)


def per_device(
    velocity, forward_now, forward_before, adjoint_now, adjoint_after,
    source_cells, receiver_cells, wavelet, observed,
):
    index_x = lax.axis_index("gx")
    index_y = lax.axis_index("gy")
    base = jnp.stack([index_x * OWN, index_y * OWN]).astype(jnp.int32)
    everywhere = ("gx", "gy")

    padded = jnp.pad(velocity, ((0, 0), (3, 4), (0, 0)))
    windows = jnp.stack([padded[:, 10 * j : 10 * j + 17].reshape(-1) for j in range(16)])
    windows = jnp.broadcast_to(windows[None], (8, 16, 680)).reshape(128, 680)
    arrived = lax.all_to_all(windows, everywhere, 0, 0, tiled=True)
    arrived = jnp.pad(arrived.reshape(8, 16, 680), ((0, 0), (1, 1), (0, 0)))
    arrived = lax.dynamic_slice_in_dim(arrived, 2 * index_x, 4, axis=1)
    arrived = arrived.reshape(8, 20, 17, 8).transpose(1, 2, 0, 3).reshape(20, 17, 64)
    model = jnp.pad(arrived, ((0, 0), (0, 7), (0, 0)))

    forward_pieces = exchange(forward_now, forward_before)
    adjoint_pieces = exchange(adjoint_now, adjoint_after)

    own_list, ext_list, counts = pl.pallas_call(
        list_kernel,
        out_shape=(
            jax.ShapeDtypeStruct((1024,), jnp.int32),
            jax.ShapeDtypeStruct((1024,), jnp.int32),
            jax.ShapeDtypeStruct((2,), jnp.int32),
        ),
        in_specs=[spec(SMEM)] * 2,
        out_specs=(spec(SMEM),) * 3,
        cost_estimate=pl.CostEstimate(flops=10_000_000, bytes_accessed=20_000_000, transcendentals=0),
    )(base, receiver_cells.reshape(-1))

    courant, inverse = pl.pallas_call(
        model_kernel,
        out_shape=(
            jax.ShapeDtypeStruct((EXT, 2, EXT, LANES), jnp.float32),
            jax.ShapeDtypeStruct((OWN, 2, OWN, LANES), jnp.float32),
        ),
        in_specs=[spec(SMEM), spec(VMEM)],
        out_specs=(spec(VMEM), spec(VMEM)),
        scratch_shapes=[VMEM((20, 2, EXT, LANES), jnp.float32)],
        compiler_params=params(32),
        cost_estimate=pl.CostEstimate(flops=10_000_000, bytes_accessed=10_000_000, transcendentals=0),
    )(base, model)

    field = VMEM((EXT, 2, EXT, LANES), jnp.float32)
    accel_shape = (ITERS, ACC_PLANES, 2, ACC_ROWS, LANES)
    matrix = z_matrix()
    accel, residual = pl.pallas_call(
        forward_kernel,
        out_shape=(
            jax.ShapeDtypeStruct(accel_shape, jnp.float32),
            jax.ShapeDtypeStruct((ITERS, 8, LANES), jnp.float32),
        ),
        in_specs=[spec(SMEM)] * 5 + [spec(VMEM)] * 3 + [spec(pl.ANY)] * 9,
        out_specs=(spec(pl.ANY), spec(VMEM)),
        scratch_shapes=[field] * 5 + [VMEM(accel_shape, jnp.float32), pltpu.SemaphoreType.DMA((2,))],
        compiler_params=params(48),
        cost_estimate=pl.CostEstimate(flops=100_000_000, bytes_accessed=30_000_000, transcendentals=0),
    )(
        base, source_cells.reshape(-1), wavelet.reshape(-1), own_list, counts,
        receiver_cells.reshape(3, 8, LANES), observed.reshape(ITERS, 8, LANES), matrix,
        forward_now, forward_before, *forward_pieces, courant,
    )

    low, high = shifts("gx", residual, residual)
    residual = residual + low + high
    low, high = shifts("gy", residual, residual)
    residual = (residual + low + high).reshape(-1)

    part = pl.pallas_call(
        adjoint_kernel,
        out_shape=jax.ShapeDtypeStruct((11, 16, 64), jnp.float32),
        in_specs=[spec(SMEM)] * 4 + [spec(VMEM)] + [spec(pl.ANY)] * 11,
        out_specs=spec(VMEM),
        scratch_shapes=[field] * 7
        + [
            VMEM(accel_shape, jnp.float32),
            VMEM((OWN, 2, OWN, LANES), jnp.float32),
            VMEM((11, 2, OWN, LANES), jnp.float32),
            pltpu.SemaphoreType.DMA((2,)),
        ],
        compiler_params=params(58),
        cost_estimate=pl.CostEstimate(flops=100_000_000, bytes_accessed=30_000_000, transcendentals=0),
    )(
        base, ext_list, counts, residual, matrix,
        adjoint_now, adjoint_after, *adjoint_pieces, courant, accel, inverse,
    )

    spread = lax.dynamic_update_slice(
        jnp.zeros((85, 11, 64), jnp.float32), part[:, :11], (10 * index_x, 0, 0)
    )[:80]
    spread = spread.reshape(16, 5, 11, 8, 8).transpose(3, 0, 1, 2, 4).reshape(128, 440)
    returned = lax.all_to_all(spread, everywhere, 0, 0, tiled=True)
    summed = returned.reshape(8, 16, 5, 11, 8).sum(axis=0)
    main = summed[:, :, :10]
    over = jnp.pad(summed[:-1, :, 10:], ((1, 0), (0, 0), (0, 9), (0, 0)))
    return (main + over).transpose(1, 0, 2, 3).reshape(5, 160, 8)


def solution(mesh):
    return jax.shard_map(
        per_device,
        mesh=mesh,
        in_specs=(
            P("gy", None, "gx"),
            P("gx", "gy", None),
            P("gx", "gy", None),
            P("gx", "gy", None),
            P("gx", "gy", None),
            P(),
            P(),
            P(),
            P(),
        ),
        out_specs=P("gy", None, "gx"),
        check_vma=False,
    )
```

```python
import jax
import jax.numpy as jnp
from jax import lax
from jax.experimental import pallas as pl
from jax.experimental.pallas import tpu as pltpu
from jax.sharding import PartitionSpec as P

ITERS = 4
OWN = 40
HALO = 20
EXT = OWN + 2 * HALO
TOP = 24
ROWS = 96
WIDE = 72
LANES = 128
CENTRE = -43050.0
RING = (8064.0, -1008.0, 128.0, -9.0)
SCALE = 0.01 / 5040.0
SMEM = pltpu.SMEM
VMEM = pltpu.VMEM
HBM = pltpu.HBM
EXACT = lax.Precision.HIGHEST


def params(mib):
    return pltpu.CompilerParams(vmem_limit_bytes=mib * 1024 * 1024)


def cost(flops, size):
    return pl.CostEstimate(flops=flops, bytes_accessed=size, transcendentals=0)


def spec(space):
    return pl.BlockSpec(memory_space=space)


def z_matrix():
    row = lax.broadcasted_iota(jnp.int32, (512, 256), 0) & 255
    column = lax.broadcasted_iota(jnp.int32, (512, 256), 1)
    distance = jnp.abs(row - column)
    result = jnp.zeros((512, 256), jnp.float32)
    for reach, value in enumerate(RING):
        result = jnp.where(distance == reach + 1, value, result)
    return result.astype(jnp.bfloat16)


def y_matrix(rows, window):
    row = lax.broadcasted_iota(jnp.int32, (rows, 2 * window), 0)
    column = lax.broadcasted_iota(jnp.int32, (rows, 2 * window), 1) % window
    distance = jnp.abs(column - 8 - row)
    result = jnp.zeros((rows, 2 * window), jnp.float32)
    for reach, value in enumerate(RING):
        result = jnp.where(distance == reach + 1, value, result)
    return result.astype(jnp.bfloat16)


def hat(fine, coarse, lower, limit, fraction):
    higher = jnp.minimum(lower + 1, limit)
    first = jnp.where(coarse == lower, 1.0 - fraction, 0.0)
    second = jnp.where(coarse == higher, fraction, 0.0)
    return first + second


def quarter(fine):
    return (fine & 3).astype(jnp.float32) * 0.25


def start_all(pairs, sem):
    started = [pltpu.make_async_copy(a, b, sem) for a, b in pairs]
    for copy in started:
        copy.start()
    return started


def wait_all(started):
    for copy in started:
        copy.wait()


def list_kernel(code_ref, own_ref, count_ref):
    def body(receiver, own):
        code = code_ref[receiver]
        own_ref[own] = code
        return own + lax.shift_right_logical(code, 31)

    count_ref[0] = lax.fori_loop(0, 1024, body, 0, unroll=16)


def receiver_codes(cells, base):
    x = cells[0] - base[0]
    y = cells[1] - base[1]
    own = (x >= 0) & (x < OWN) & (y >= 0) & (y < OWN)
    code = jnp.arange(1024, dtype=jnp.int32) | (cells[2] << 10)
    code = code | ((y & 63) << 18) | ((x & 63) << 24)
    return code | (own.astype(jnp.int32) << 31)


def unpack(code):
    receiver = code & 1023
    z = (code >> 10) & 255
    y = (code >> 18) & 63
    x = (code >> 24) & 63
    return receiver, x + HALO, y + TOP, z // LANES, z & (LANES - 1)


def model_pack_kernel(velocity_ref, out_ref):
    lane = lax.broadcasted_iota(jnp.int32, (8, LANES), 1)
    blocks = [velocity_ref[a] for a in range(5)]
    for j in range(16):
        tile = jnp.zeros((8, LANES), jnp.float32)
        for a in range(5):
            moved = pltpu.roll(blocks[a], (24 * a - 10 * j) % 256, 1)[:, :LANES]
            tile = jnp.where((lane >= 24 * a) & (lane < 24 * a + 24), moved, tile)
        for i in range(8):
            out_ref[i, j] = tile


def model_kernel(base_ref, model_ref, plane_out, plane_ref, sem):
    row = lax.broadcasted_iota(jnp.int32, (64, 256), 0)
    column = lax.broadcasted_iota(jnp.int32, (64, 256), 1)
    weight_z = hat(column, row, column // 4, 63, quarter(column))
    fine = lax.broadcasted_iota(jnp.int32, (ROWS, 24), 0)
    coarse = lax.broadcasted_iota(jnp.int32, (ROWS, 24), 1)
    limit_y = 159 - (base_ref[1] // 4 - 4)
    weight_y = hat(fine, coarse, fine // 4 - 2, limit_y, quarter(fine))
    place = fine + (base_ref[1] - TOP)
    weight_y = jnp.where((place >= 0) & (place < 640), weight_y, 0.0)
    first = 2 * (base_ref[0] // OWN) - 1
    for r in range(4):
        owner = jnp.clip(first + r, 0, 15)
        block = jnp.concatenate([model_ref[i, owner] for i in range(8)], axis=0)
        deep = jnp.dot(block.T, weight_z, precision=EXACT, preferred_element_type=jnp.float32)
        for a in range(5):
            plane = jnp.dot(
                weight_y, deep[24 * a : 24 * a + 24], precision=EXACT,
                preferred_element_type=jnp.float32,
            )
            plane_ref[5 * r + a, 0] = plane[:, :LANES]
            plane_ref[5 * r + a, 1] = plane[:, LANES:]
    wait_all(start_all([(plane_ref, plane_out)], sem))


def fill_courant(base_ref, plane_ref, courant_ref):
    limit_x = 79 - (base_ref[0] // 4 - 5)

    def group(a, carry):
        higher = jnp.minimum(a + 1, limit_x)
        start = base_ref[0] - HALO + 4 * a
        inside = ((start >= 0) & (start < 320)).astype(jnp.float32) * SCALE
        for half in range(2):
            for tile in range(1, 10):
                rows = pl.ds(8 * tile, 8)
                low = plane_ref[a, half, rows, :]
                high = plane_ref[higher, half, rows, :]
                for step in range(4):
                    speed = low * (1.0 - 0.25 * step) + high * (0.25 * step)
                    courant_ref[4 * a + step, half, rows, :] = speed * speed * inside
        return carry

    lax.fori_loop(1, 19, group, 0)


def clear(ref, planes, tiles):
    def body(x, carry):
        for half in range(2):
            for tile in tiles:
                ref[x, half, pl.ds(8 * tile, 8), :] = jnp.zeros((8, LANES), jnp.float32)
        return carry

    lax.fori_loop(planes[0], planes[1], body, 0)


def clear_edges(ref):
    outer = (0, 1, 2, 8, 9, 10, 11)
    clear(ref, (0, HALO), outer)
    clear(ref, (HALO, HALO + OWN), (0, 10, 11))
    clear(ref, (HALO + OWN, EXT), outer)


def copies(now, before, pieces, ext_now, ext_before):
    x_low, x_high, y_low, y_high, c_low, c_high = pieces
    result = []
    for half in range(2):
        lanes = pl.ds(half * LANES, LANES)

        def add(source, plane, count, row, rows, target, to_plane, to_row):
            result.append((
                source.at[pl.ds(plane, count), pl.ds(row, rows), lanes],
                target.at[pl.ds(to_plane, count), half, pl.ds(to_row, rows), :],
            ))

        add(now, 0, OWN, 0, OWN, ext_now, HALO, TOP)
        add(before, 0, OWN, 0, OWN, ext_before, HALO, TOP)
        for source, first, second in ((x_low, 0, 4), (x_high, 60, 60)):
            add(source, 0, 20, 0, OWN, ext_now, first, TOP)
            add(source, 20, 16, 0, OWN, ext_before, second, TOP)
        for source, first, second in ((y_low, 0, 8), (y_high, 64, 64)):
            add(source, 0, OWN, 0, 24, ext_now, HALO, first)
            add(source, 0, OWN, 24, 16, ext_before, HALO, second)
        for piece, near, far in ((c_low, 16, 8), (c_high, 64, 72)):
            for side, places in ((0, (4, 12, 8, 16)), (40, (60, 60, 60, 60))):
                add(piece, side, 16, 0, 8, ext_now, places[0], near)
                add(piece, side + 16, 8, 0, 8, ext_now, places[1], far)
                add(piece, side + 24, 12, 0, 8, ext_before, places[2], near)
                add(piece, side + 36, 4, 0, 8, ext_before, places[3], far)
    return result


def stencil_pass(source, z_ref, y_refs, along, step, emit):
    first = 4 * step
    top = 4 + 4 * step
    span = EXT - 8 * step
    tiles = span // 8
    y_ref, window_rows = ((y_refs[0], 96), (y_refs[1], 80), (y_refs[1], 80), (y_refs[2], 64))[
        step - 1
    ]

    def multiply(x):
        parts = []
        for g in range(4):
            plane = jnp.concatenate(
                [source[x + g, half, pl.ds(top - 8, window_rows), :] for half in range(2)], axis=1
            )
            upper = plane.astype(jnp.bfloat16)
            lower = (plane - upper.astype(jnp.float32)).astype(jnp.bfloat16)
            parts.append((upper, lower))
        stacked = jnp.concatenate(
            [jnp.concatenate([part[side] for part in parts], axis=0) for side in range(2)], axis=1
        )
        along_z = jnp.dot(stacked, z_ref[...], preferred_element_type=jnp.float32)
        for g in range(4):
            along_y = jnp.dot(
                y_ref[...], jnp.concatenate(parts[g], axis=0), preferred_element_type=jnp.float32
            )
            for tile in range(tiles):
                start = g * window_rows + 8 + 8 * tile
                total = along_z[start : start + 8] + along_y[8 * tile : 8 * tile + 8]
                for half in range(2):
                    along[g, half, pl.ds(8 * tile, 8), :] = total[
                        :, half * LANES : (half + 1) * LANES
                    ]

    multiply(first)

    def group(index, carry):
        x = first + 4 * index
        for tile in range(tiles):
            for half in range(2):
                row = top + 8 * tile
                window = [source[x - 4 + j, half, pl.ds(row, 8), :] for j in range(12)]
                for g in range(4):
                    total = along[g, half, pl.ds(8 * tile, 8), :] + CENTRE * window[4 + g]
                    for reach in range(1, 5):
                        pair = window[4 + g + reach] + window[4 + g - reach]
                        total = total + RING[reach - 1] * pair
                    emit(x + g, half, row, window[4 + g], total)
        multiply(x + 4)
        return carry

    lax.fori_loop(0, span // 4, group, 0)


def propagate_kernel(
    base_ref, source_ref, wavelet_ref, own_ref, count_ref, observed_ref,
    z_ref, y_ref_a, y_ref_b, y_ref_c,
    now, before, adjoint_now, adjoint_after, *refs,
):
    pieces, refs = refs[:6], refs[6:]
    (
        plane_in, out_ref,
        field_a, field_b, field_c, stage, courant, term_a, term_b, term_c, term_d,
        planes, along, picked, sems,
    ) = refs
    terms = (term_a, term_b, term_c, term_d)
    matrices = (y_ref_a, y_ref_b, y_ref_c)
    first = start_all([(plane_in, planes)], sems.at[0])
    clear_edges(field_a)
    clear_edges(field_b)
    loads = start_all(copies(now, before, pieces, field_b, field_a), sems.at[1])
    clear(field_c, (0, EXT), range(12))
    own = pl.ds(HALO, OWN)
    later = []
    for half in range(2):
        lanes = pl.ds(half * LANES, LANES)
        later += [
            (adjoint_now.at[:, :, lanes], field_c.at[own, half, pl.ds(TOP, OWN), :]),
            (adjoint_after.at[:, :, lanes], stage.at[:, half]),
        ]
    later = start_all(later, sems.at[2])
    clear(term_b, (0, 64), (0, 8))
    clear(term_d, (0, 48), (1, 7))
    wait_all(first)
    fill_courant(base_ref, planes, courant)
    wait_all(loads)
    lane = lax.broadcasted_iota(jnp.int32, (1, LANES), 1)
    number = count_ref[0]

    for step in range(1, ITERS + 1):
        target, newer = (field_a, field_b) if step % 2 else (field_b, field_a)
        term = terms[step - 1]
        origin = 4 * step
        span = EXT - 8 * step

        def emit(x, half, row, centre, total):
            rows = pl.ds(row, 8)
            term[x - origin, half, pl.ds(row - 8, 8), :] = total
            target[x, half, rows, :] = (
                centre + centre - target[x, half, rows, :] + courant[x, half, rows, :] * total
            )

        stencil_pass(newer, z_ref, matrices, along, step, emit)
        for source in range(4):
            x = source_ref[source] - (base_ref[0] - HALO)
            row = source_ref[4 + source] - (base_ref[1] - TOP)
            z = source_ref[8 + source]
            inside_x = (x >= origin) & (x < origin + span)
            inside_y = (row >= origin + 4) & (row < origin + 4 + span)

            @pl.when(inside_x & inside_y)
            def _():
                half = z // LANES
                added = jnp.where(
                    lane == (z & (LANES - 1)), wavelet_ref[4 * (step - 1) + source], 0.0
                )
                target[x, half, pl.ds(row, 1), :] += added
                term[x - origin, half, pl.ds(row - 8, 1), :] += (
                    added / courant[x, half, pl.ds(row, 1), :]
                )

        def sample(index, carry):
            for j in range(4):
                entry = 4 * index + j
                valid = entry < number
                code = jnp.where(valid, own_ref[jnp.minimum(entry, 1023)], 0)
                receiver, x, row, half, z = unpack(code)
                at_lane = lane == jnp.where(valid, z, -1)
                line = target[x, half, pl.ds(row, 1), :]
                seen = observed_ref[1024 * (step - 1) + receiver]
                picked[step - 1, pl.ds(entry, 1), :] = jnp.where(at_lane, line - seen, 0.0)
            return carry

        lax.fori_loop(0, (number + 3) // 4, sample, 0)

    clear(field_a, (0, EXT), range(12))
    clear(field_b, (0, EXT), range(12))
    wait_all(later)

    def scale(index, carry):
        x = index + HALO
        for half in range(2):
            for tile in range(5):
                rows = pl.ds(TOP + 8 * tile, 8)
                factor = courant[x, half, rows, :]
                field_c[x, half, rows, :] = field_c[x, half, rows, :] * factor
                field_a[x, half, rows, :] = stage[index, half, pl.ds(8 * tile, 8), :] * factor
        return carry

    lax.fori_loop(0, OWN, scale, 0)
    chain = ((field_c, field_a, field_a), (field_a, field_c, field_c), (field_c, field_a, field_b))
    for step in range(ITERS, 1, -1):
        newer, older, target = chain[ITERS - step]

        def emit(x, half, row, centre, total):
            rows = pl.ds(row, 8)
            target[x, half, rows, :] = (
                centre + centre - older[x, half, rows, :] + courant[x, half, rows, :] * total
            )

        stencil_pass(newer, z_ref, matrices, along, step, emit)

        def inject(entry, carry):
            _, x, row, half, _ = unpack(own_ref[entry])
            rows = pl.ds(row, 1)
            target[x, half, rows, :] += (
                courant[x, half, rows, :] * picked[step - 1, pl.ds(entry, 1), :]
            )
            return carry

        lax.fori_loop(0, number, inject, 0)

    def prepare(entry, carry):
        _, x, row, half, _ = unpack(own_ref[entry])
        rows = pl.ds(row, 1)
        picked[0, pl.ds(entry, 1), :] = (
            picked[0, pl.ds(entry, 1), :]
            * courant[x, half, rows, :]
            * term_a[x - 4, half, pl.ds(row - 8, 1), :]
        )
        return carry

    lax.fori_loop(0, number, prepare, 0)

    def emit(x, half, row, centre, total):
        rows, place = pl.ds(row, 8), pl.ds(row - 8, 8)
        value = centre + centre - field_c[x, half, rows, :] + courant[x, half, rows, :] * total
        term_a[x - 4, half, place, :] = value * term_a[x - 4, half, place, :]

    stencil_pass(field_b, z_ref, matrices, along, 1, emit)

    def finish(entry, carry):
        _, x, row, half, _ = unpack(own_ref[entry])
        term_a[x - 4, half, pl.ds(row - 8, 1), :] += picked[0, pl.ds(entry, 1), :]
        return carry

    lax.fori_loop(0, number, finish, 0)

    coarse = planes
    clear(coarse, (0, 20), range(9))
    limit_x = 79 - (base_ref[0] // 4 - 4)

    def image(a, carry):
        higher = jnp.clip(limit_x, 0, a + 1)
        for half in range(2):
            for tile in range(9):
                rows, place = pl.ds(8 + 8 * tile, 8), pl.ds(8 * tile, 8)
                low, high = None, None
                for g in range(4):
                    x = 4 + 4 * a + g
                    total = term_a[x - 4, half, place, :] + (
                        field_b[x, half, rows, :]
                        * term_b[jnp.clip(x - 8, 0, 63), half, place, :]
                    )
                    if 0 < tile < 8:
                        total = total + (
                            field_c[x, half, rows, :]
                            * term_c[jnp.clip(x - 12, 0, 55), half, place, :]
                        )
                        total = total + (
                            field_a[x, half, rows, :]
                            * term_d[jnp.clip(x - 16, 0, 47), half, place, :]
                        )
                    total = total * lax.rsqrt(jnp.maximum(courant[x, half, rows, :], 1e-9))
                    weight = 0.25 * g
                    low = total if low is None else low + (1.0 - weight) * total
                    if g:
                        part = weight * total
                        high = part if high is None else high + part
                coarse[a, half, place, :] += low
                coarse[higher, half, place, :] += high
        return carry

    lax.fori_loop(0, 18, image, 0)
    row = lax.broadcasted_iota(jnp.int32, (24, WIDE), 0)
    fine = lax.broadcasted_iota(jnp.int32, (24, WIDE), 1)
    limit_y = 159 - (base_ref[1] // 4 - 4)
    weight_y = hat(fine, row, fine // 4, limit_y, quarter(fine))
    column = lax.broadcasted_iota(jnp.int32, (64, 256), 0)
    fine = lax.broadcasted_iota(jnp.int32, (64, 256), 1)
    weight_z = hat(fine, column, fine // 4, 63, quarter(fine))
    parts = [jnp.zeros((24, 256), jnp.float32)]
    for a in range(19):
        plane = jnp.concatenate(
            [coarse[a, half, pl.ds(0, WIDE), :] for half in range(2)], axis=1
        )
        parts.append(
            jnp.dot(weight_y, plane, precision=EXACT, preferred_element_type=jnp.float32)
        )
    parts.append(jnp.zeros((32, 256), jnp.float32))
    result = (0.125 * 2.0 * SCALE**0.5) * lax.dot_general(
        weight_z, jnp.concatenate(parts, axis=0), (((1,), (1,)), ((), ())),
        precision=EXACT, preferred_element_type=jnp.float32,
    )
    out_ref[...] = jnp.zeros(out_ref.shape, jnp.float32)
    index = base_ref[0] // OWN
    for piece in range(4):
        owner = 2 * index - 1 + piece

        @pl.when((owner >= 0) & (owner < 16))
        def _():
            moved = pltpu.roll(result, (512 - 120 * piece) % 512, 1) if piece else result
            for i in range(8):
                out_ref[i, owner] = moved[8 * i : 8 * i + 8, :LANES]


def gather_kernel(base_ref, parts_ref, out_ref):
    wide = lax.broadcasted_iota(jnp.int32, (8, 256), 1)
    index = base_ref[1] // OWN
    one = index // 2
    other = jnp.where(index % 2 == 0, one - 1, one + 1)
    valid = (other >= 0) & (other < 8)
    other = jnp.clip(other, 0, 7)
    sums = [jnp.zeros((8, 256), jnp.float32) for _ in range(5)]
    for j in range(16):
        tile = parts_ref[one, j] + jnp.where(valid, parts_ref[other, j], 0.0)
        tile = jnp.concatenate([tile, jnp.zeros((8, LANES), jnp.float32)], axis=1)
        inside = (wide >= 10 * j - 4) & (wide < 10 * j + 15)
        for r in range(5):
            moved = pltpu.roll(tile, (10 * j - 4 - 24 * r) % 256, 1)
            sums[r] = sums[r] + jnp.where(inside, moved, 0.0)
    for r in range(5):
        out_ref[r] = sums[r]


def face_kernel(now, before, *refs):
    outs, stages, sem = refs[:4], refs[4:8], refs[8]
    pairs = []
    for side, (first, second, strip_first) in enumerate(((20, 24, 16), (0, 0, 0))):
        face, strip = stages[side], stages[2 + side]
        pairs += [
            (now.at[pl.ds(first, 20)], face.at[pl.ds(0, 20)]),
            (before.at[pl.ds(second, 16)], face.at[pl.ds(20, 16)]),
            (now.at[:, pl.ds(strip_first, 24)], strip.at[:, pl.ds(0, 24)]),
            (before.at[:, pl.ds(second, 16)], strip.at[:, pl.ds(24, 16)]),
        ]
    wait_all(start_all(pairs, sem))
    wait_all(start_all(list(zip(stages, outs)), sem))


def corner_kernel(x_low, x_high, up, down, stage_up, stage_down, sem):
    pairs = []
    for target, near, far in ((stage_up, 32, 24), (stage_down, 0, 8)):
        for piece, start, places in ((x_low, 0, (4, 12, 24, 32)), (x_high, 40, (0, 0, 20, 20))):
            place = start
            for plane, row, count in zip(places, (near, far, near, far), (16, 8, 12, 4)):
                pairs.append((
                    piece.at[pl.ds(plane, count), pl.ds(row, 8)],
                    target.at[pl.ds(place, count)],
                ))
                place += count
    wait_all(start_all(pairs, sem))
    wait_all(start_all([(stage_up, up), (stage_down, down)], sem))


def gate_kernel(*refs):
    pass


def gate(arrays, tokens):
    return pl.pallas_call(
        gate_kernel,
        out_shape=tuple(jax.ShapeDtypeStruct(a.shape, a.dtype) for a in arrays),
        in_specs=[spec(HBM)] * len(arrays) + [spec(pl.ANY)] * len(tokens),
        out_specs=(spec(HBM),) * len(arrays),
        input_output_aliases={i: i for i in range(len(arrays))},
        cost_estimate=cost(1000, 1000),
    )(*arrays, *tokens)


def shifts(axis, block_up, block_down):
    count = lax.axis_size(axis)
    up = [(i, i + 1) for i in range(count - 1)]
    down = [(i + 1, i) for i in range(count - 1)]
    return lax.ppermute(block_up, axis, up), lax.ppermute(block_down, axis, down)


def staged(kernel, shapes, operands, size):
    shapes = tuple(jax.ShapeDtypeStruct(shape, jnp.float32) for shape in shapes)
    return pl.pallas_call(
        kernel,
        out_shape=shapes,
        in_specs=[spec(HBM)] * len(operands),
        out_specs=(spec(HBM),) * len(shapes),
        scratch_shapes=[VMEM(shape.shape, shape.dtype) for shape in shapes]
        + [pltpu.SemaphoreType.DMA],
        cost_estimate=cost(1000, size),
    )(*operands)


def per_device(
    velocity, forward_now, forward_before, adjoint_now, adjoint_after,
    source_cells, receiver_cells, wavelet, observed,
):
    index_x = lax.axis_index("gx")
    index_y = lax.axis_index("gy")
    base = jnp.stack([index_x * OWN, index_y * OWN]).astype(jnp.int32)
    everywhere = ("gx", "gy")
    buffer = jax.ShapeDtypeStruct((8, 16, 8, LANES), jnp.float32)

    turned = jnp.pad(velocity.transpose(0, 2, 1), ((0, 0), (0, 0), (4, 92)))
    windows = pl.pallas_call(
        model_pack_kernel,
        out_shape=buffer,
        in_specs=[spec(VMEM)],
        out_specs=spec(VMEM),
        cost_estimate=cost(100_000, 600_000),
    )(turned)
    model = lax.all_to_all(windows.reshape(128, 8, LANES), everywhere, 0, 0, tiled=True)
    model = model.reshape(8, 16, 8, LANES)

    own_list, counts = pl.pallas_call(
        list_kernel,
        out_shape=(
            jax.ShapeDtypeStruct((1024,), jnp.int32),
            jax.ShapeDtypeStruct((1,), jnp.int32),
        ),
        in_specs=[spec(SMEM)],
        out_specs=(spec(SMEM),) * 2,
        cost_estimate=cost(10_000_000, 20_000_000),
    )(receiver_codes(receiver_cells, base))

    faces = staged(
        face_kernel, ((36, OWN, 256),) * 2 + ((OWN, 40, 256),) * 2,
        (forward_now, forward_before), 9_000_000,
    )
    x_up, x_down, y_up, y_down = gate(faces, (windows,))
    x_low, x_high = shifts("gx", x_up, x_down)
    y_low, y_high = shifts("gy", y_up, y_down)

    plane_shape = (20, 2, ROWS, LANES)
    planes = pl.pallas_call(
        model_kernel,
        out_shape=jax.ShapeDtypeStruct(plane_shape, jnp.float32),
        in_specs=[spec(SMEM), spec(VMEM)],
        out_specs=spec(HBM),
        scratch_shapes=[VMEM(plane_shape, jnp.float32), pltpu.SemaphoreType.DMA],
        compiler_params=params(32),
        cost_estimate=cost(10_000_000, 10_000_000),
    )(base, model)

    corners = staged(corner_kernel, ((80, 8, 256),) * 2, (x_low, x_high), 2_000_000)
    c_low, c_high = shifts("gy", *corners)

    field = VMEM((EXT, 2, ROWS, LANES), jnp.float32)
    parts = pl.pallas_call(
        propagate_kernel,
        out_shape=buffer,
        in_specs=[spec(SMEM)] * 6 + [spec(VMEM)] * 4 + [spec(HBM)] * 11,
        out_specs=spec(VMEM),
        scratch_shapes=[
            field, field, field,
            VMEM((OWN, 2, OWN, LANES), jnp.float32),
            field,
            *(VMEM((EXT - 8 * s, 2, WIDE, LANES), jnp.float32) for s in range(1, 5)),
            VMEM(plane_shape, jnp.float32),
            VMEM((4, 2, WIDE, LANES), jnp.float32),
            VMEM((ITERS, 1024, LANES), jnp.float32),
            pltpu.SemaphoreType.DMA((3,)),
        ],
        compiler_params=params(60),
        cost_estimate=cost(200_000_000, 30_000_000),
    )(
        base, source_cells.reshape(-1), wavelet.reshape(-1), own_list, counts,
        observed.reshape(-1), z_matrix(), y_matrix(80, 96), y_matrix(64, 80), y_matrix(48, 64),
        forward_now, forward_before, adjoint_now, adjoint_after,
        x_low, x_high, y_low, y_high, c_low, c_high, planes,
    )

    parts = lax.all_to_all(parts.reshape(128, 8, LANES), everywhere, 0, 0, tiled=True)
    grid = pl.pallas_call(
        gather_kernel,
        out_shape=jax.ShapeDtypeStruct((5, 8, 256), jnp.float32),
        in_specs=[spec(SMEM), spec(VMEM)],
        out_specs=spec(VMEM),
        cost_estimate=cost(100_000, 600_000),
    )(base, parts.reshape(8, 16, 8, LANES))
    return grid[:, :, :160].transpose(0, 2, 1)


def solution(mesh):
    return jax.shard_map(
        per_device,
        mesh=mesh,
        in_specs=(
            P("gy", None, "gx"),
            P("gx", "gy", None),
            P("gx", "gy", None),
            P("gx", "gy", None),
            P("gx", "gy", None),
            P(),
            P(),
            P(),
            P(),
        ),
        out_specs=P("gy", None, "gx"),
        check_vma=False,
    )
```

```python
import jax
import jax.numpy as jnp
from jax import lax
from jax.experimental import pallas as pl
from jax.experimental.pallas import tpu as pltpu
from jax.sharding import PartitionSpec as P

ITERS = 4
OWN = 40
HALO = 20
SPLIT = 40
EXT = OWN + 2 * HALO
TOP = 24
ROWS = 96
WIDE = 72
LANES = 128
CENTRE = -43050.0
RING = (8064.0, -1008.0, 128.0, -9.0)
SCALE = 0.01 / 5040.0
SMEM = pltpu.SMEM
VMEM = pltpu.VMEM
HBM = pltpu.HBM
EXACT = lax.Precision.HIGHEST


def params(mib):
    return pltpu.CompilerParams(vmem_limit_bytes=mib * 1024 * 1024)


def cost(flops, size):
    return pl.CostEstimate(flops=flops, bytes_accessed=size, transcendentals=0)


def spec(space):
    return pl.BlockSpec(memory_space=space)


def z_matrix():
    row = lax.broadcasted_iota(jnp.int32, (256, 256), 0)
    column = lax.broadcasted_iota(jnp.int32, (256, 256), 1)
    distance = jnp.abs(row - column)
    result = jnp.zeros((256, 256), jnp.float32)
    for reach, value in enumerate(RING):
        result = jnp.where(distance == reach + 1, value, result)
    return result.astype(jnp.bfloat16)


def y_matrix(rows, window):
    row = lax.broadcasted_iota(jnp.int32, (rows, 2 * window), 0)
    column = lax.broadcasted_iota(jnp.int32, (rows, 2 * window), 1) % window
    distance = jnp.abs(column - 8 - row)
    result = jnp.zeros((rows, 2 * window), jnp.float32)
    for reach, value in enumerate(RING):
        result = jnp.where(distance == reach + 1, value, result)
    return result.astype(jnp.bfloat16)


def hat(fine, coarse, lower, limit, fraction):
    higher = jnp.minimum(lower + 1, limit)
    first = jnp.where(coarse == lower, 1.0 - fraction, 0.0)
    second = jnp.where(coarse == higher, fraction, 0.0)
    return first + second


def quarter(fine):
    return (fine & 3).astype(jnp.float32) * 0.25


def start_all(pairs, sem):
    started = [pltpu.make_async_copy(a, b, sem) for a, b in pairs]
    for copy in started:
        copy.start()
    return started


def wait_all(started):
    for copy in started:
        copy.wait()


def list_kernel(code_ref, own_ref, count_ref):
    def body(receiver, own):
        code = code_ref[receiver]
        own_ref[own] = code
        return own + lax.shift_right_logical(code, 31)

    count_ref[0] = lax.fori_loop(0, 1024, body, 0, unroll=16)


def receiver_codes(cells, base):
    x = cells[0] - base[0]
    y = cells[1] - base[1]
    own = (x >= 0) & (x < OWN) & (y >= 0) & (y < OWN)
    code = jnp.arange(1024, dtype=jnp.int32) | (cells[2] << 10)
    code = code | ((y & 63) << 18) | ((x & 63) << 24)
    return code | (own.astype(jnp.int32) << 31)


def unpack(code):
    receiver = code & 1023
    z = (code >> 10) & 255
    y = (code >> 18) & 63
    x = (code >> 24) & 63
    return receiver, x + HALO, y + TOP, z // LANES, z & (LANES - 1)


def model_pack_kernel(velocity_ref, out_ref):
    lane = lax.broadcasted_iota(jnp.int32, (8, LANES), 1)
    blocks = [velocity_ref[a] for a in range(5)]
    for j in range(16):
        tile = jnp.zeros((8, LANES), jnp.float32)
        for a in range(5):
            moved = pltpu.roll(blocks[a], (24 * a - 10 * j) % 256, 1)[:, :LANES]
            tile = jnp.where((lane >= 24 * a) & (lane < 24 * a + 24), moved, tile)
        for i in range(8):
            out_ref[i, j] = tile


def model_kernel(base_ref, model_ref, plane_out, plane_ref, sem):
    row = lax.broadcasted_iota(jnp.int32, (64, 256), 0)
    column = lax.broadcasted_iota(jnp.int32, (64, 256), 1)
    weight_z = hat(column, row, column // 4, 63, quarter(column))
    fine = lax.broadcasted_iota(jnp.int32, (ROWS, 24), 0)
    coarse = lax.broadcasted_iota(jnp.int32, (ROWS, 24), 1)
    limit_y = 159 - (base_ref[1] // 4 - 4)
    weight_y = hat(fine, coarse, fine // 4 - 2, limit_y, quarter(fine))
    place = fine + (base_ref[1] - TOP)
    weight_y = jnp.where((place >= 0) & (place < 640), weight_y, 0.0)
    first = 2 * (base_ref[0] // OWN) - 1
    for r in range(4):
        owner = jnp.clip(first + r, 0, 15)
        block = jnp.concatenate([model_ref[i, owner] for i in range(8)], axis=0)
        deep = jnp.dot(block.T, weight_z, precision=EXACT, preferred_element_type=jnp.float32)
        for a in range(5):
            plane = jnp.dot(
                weight_y, deep[24 * a : 24 * a + 24], precision=EXACT,
                preferred_element_type=jnp.float32,
            )
            plane_ref[5 * r + a, 0] = plane[:, :LANES]
            plane_ref[5 * r + a, 1] = plane[:, LANES:]
    wait_all(start_all([(plane_ref, plane_out)], sem))


def fill_courant(base_ref, plane_ref, courant_ref):
    limit_x = 79 - (base_ref[0] // 4 - 5)

    def group(a, carry):
        higher = jnp.minimum(a + 1, limit_x)
        start = base_ref[0] - HALO + 4 * a
        inside = ((start >= 0) & (start < 320)).astype(jnp.float32) * SCALE
        for half in range(2):
            for tile in range(1, 10):
                rows = pl.ds(8 * tile, 8)
                low = plane_ref[a, half, rows, :]
                high = plane_ref[higher, half, rows, :]
                for step in range(4):
                    speed = low * (1.0 - 0.25 * step) + high * (0.25 * step)
                    courant_ref[4 * a + step, half, rows, :] = speed * speed * inside
        return carry

    lax.fori_loop(1, 19, group, 0)


def clear(ref, planes, tiles):
    def body(x, carry):
        for half in range(2):
            for tile in tiles:
                ref[x, half, pl.ds(8 * tile, 8), :] = jnp.zeros((8, LANES), jnp.float32)
        return carry

    lax.fori_loop(planes[0], planes[1], body, 0)


def clear_edges(ref):
    outer = (0, 1, 2, 8, 9, 10, 11)
    clear(ref, (0, HALO), outer)
    clear(ref, (HALO, HALO + OWN), (0, 10, 11))
    clear(ref, (HALO + OWN, EXT), outer)


def copies(now, before, pieces, ext_now, ext_before):
    x_low, x_high, y_low, y_high, c_low, c_high = pieces
    early, late = [], []
    for half in range(2):
        lanes = pl.ds(half * LANES, LANES)

        def add(source, plane, count, row, rows, target, to_plane, to_row):
            (early if to_plane < SPLIT else late).append((
                source.at[pl.ds(plane, count), pl.ds(row, rows), lanes],
                target.at[pl.ds(to_plane, count), half, pl.ds(to_row, rows), :],
            ))

        for plane in (0, SPLIT - HALO):
            place = plane + HALO
            add(now, plane, 20, 0, OWN, ext_now, place, TOP)
            add(before, plane, 20, 0, OWN, ext_before, place, TOP)
            for source, first, second in ((y_low, 0, 8), (y_high, 64, 64)):
                add(source, plane, 20, 0, 24, ext_now, place, first)
                add(source, plane, 20, 24, 16, ext_before, place, second)
        for source, first, second in ((x_low, 0, 4), (x_high, 60, 60)):
            add(source, 0, 20, 0, OWN, ext_now, first, TOP)
            add(source, 20, 16, 0, OWN, ext_before, second, TOP)
        for piece, near, far in ((c_low, 16, 8), (c_high, 64, 72)):
            for side, places in ((0, (4, 12, 8, 16)), (40, (60, 60, 60, 60))):
                add(piece, side, 16, 0, 8, ext_now, places[0], near)
                add(piece, side + 16, 8, 0, 8, ext_now, places[1], far)
                add(piece, side + 24, 12, 0, 8, ext_before, places[2], near)
                add(piece, side + 36, 4, 0, 8, ext_before, places[3], far)
    return early, late


def stencil_pass(source, z_ref, y_refs, step, emit, wait_late=None):
    first = 4 * step
    top = 4 + 4 * step
    span = EXT - 8 * step
    tiles = span // 8
    keep = -(-(8 + span) // 16) * 16
    y_ref, window_rows = ((y_refs[0], 96), (y_refs[1], 80), (y_refs[1], 80), (y_refs[2], 64))[
        step - 1
    ]

    def multiply(x):
        parts = []
        kept = {}
        for g in range(8):
            plane = jnp.concatenate(
                [source[x + g, half, pl.ds(top - 8, window_rows), :] for half in range(2)], axis=1
            )
            upper = plane.astype(jnp.bfloat16)
            lower = (plane - upper.astype(jnp.float32)).astype(jnp.bfloat16)
            parts.append((upper, lower))
        along_z = []
        for pair in (parts[:2], parts[2:4], parts[4:6], parts[6:]):
            stacked = jnp.concatenate(
                [part[side][:keep] for side in range(2) for part in pair], axis=0
            )
            both = jnp.dot(stacked, z_ref[...], preferred_element_type=jnp.float32)
            along_z.append(both[: 2 * keep] + both[2 * keep :])
        for g in range(8):
            along_y = jnp.dot(
                y_ref[...], jnp.concatenate(parts[g], axis=0), preferred_element_type=jnp.float32
            )
            for tile in range(tiles):
                start = (g % 2) * keep + 8 + 8 * tile
                total = along_z[g // 2][start : start + 8] + along_y[8 * tile : 8 * tile + 8]
                for half in range(2):
                    kept[g, tile, half] = total[:, half * LANES : (half + 1) * LANES]
        return kept

    def group(index, carry):
        if wait_late is not None:
            pl.when(index == (SPLIT - 16) // 8)(wait_late)
        x = first + 8 * index
        kept = multiply(x)
        for tile in range(tiles):
            for half in range(2):
                row = top + 8 * tile
                for g in range(8):
                    window = [source[x + g - 4 + j, half, pl.ds(row, 8), :] for j in range(9)]
                    total = CENTRE * window[4]
                    for reach in range(1, 5):
                        total = total + RING[reach - 1] * (window[4 + reach] + window[4 - reach])
                    total = total + kept[g, tile, half]
                    emit(x + g, half, row, window[4], total)
        return carry

    lax.fori_loop(0, span // 8, group, 0)


def propagate_kernel(
    base_ref, source_ref, wavelet_ref, own_ref, count_ref, observed_ref,
    z_ref, y_ref_a, y_ref_b, y_ref_c,
    now, before, adjoint_now, adjoint_after, *refs,
):
    pieces, refs = refs[:6], refs[6:]
    (
        plane_in, out_ref,
        field_a, field_b, field_c, stage, courant, term_a, term_b, term_c, term_d,
        planes, picked, sems,
    ) = refs
    terms = (term_a, term_b, term_c, term_d)
    matrices = (y_ref_a, y_ref_b, y_ref_c)
    first = start_all([(plane_in, planes)], sems.at[0])
    clear_edges(field_a)
    clear_edges(field_b)
    early, late = copies(now, before, pieces, field_b, field_a)
    early = start_all(early, sems.at[1])
    late = start_all(late, sems.at[2])
    clear(field_c, (0, EXT), range(12))
    own = pl.ds(HALO, OWN)
    later = []
    for half in range(2):
        lanes = pl.ds(half * LANES, LANES)
        later += [
            (adjoint_now.at[:, :, lanes], field_c.at[own, half, pl.ds(TOP, OWN), :]),
            (adjoint_after.at[:, :, lanes], stage.at[:, half]),
        ]
    later = start_all(later, sems.at[3])
    clear(term_b, (0, 64), (0, 8))
    clear(term_d, (0, 48), (1, 7))
    wait_all(first)
    fill_courant(base_ref, planes, courant)
    wait_all(early)
    lane = lax.broadcasted_iota(jnp.int32, (1, LANES), 1)
    number = count_ref[0]

    for step in range(1, ITERS + 1):
        target, newer = (field_a, field_b) if step % 2 else (field_b, field_a)
        term = terms[step - 1]
        origin = 4 * step
        span = EXT - 8 * step

        def emit(x, half, row, centre, total):
            rows = pl.ds(row, 8)
            term[x - origin, half, pl.ds(row - 8, 8), :] = total
            target[x, half, rows, :] = (
                centre + centre - target[x, half, rows, :] + courant[x, half, rows, :] * total
            )

        stencil_pass(
            newer, z_ref, matrices, step, emit,
            (lambda: wait_all(late)) if step == 1 else None,
        )
        for source in range(4):
            x = source_ref[source] - (base_ref[0] - HALO)
            row = source_ref[4 + source] - (base_ref[1] - TOP)
            z = source_ref[8 + source]
            inside_x = (x >= origin) & (x < origin + span)
            inside_y = (row >= origin + 4) & (row < origin + 4 + span)

            @pl.when(inside_x & inside_y)
            def _():
                half = z // LANES
                added = jnp.where(
                    lane == (z & (LANES - 1)), wavelet_ref[4 * (step - 1) + source], 0.0
                )
                target[x, half, pl.ds(row, 1), :] += added
                term[x - origin, half, pl.ds(row - 8, 1), :] += (
                    added / courant[x, half, pl.ds(row, 1), :]
                )

        def sample(index, carry):
            for j in range(4):
                entry = 4 * index + j
                valid = entry < number
                code = jnp.where(valid, own_ref[jnp.minimum(entry, 1023)], 0)
                receiver, x, row, half, z = unpack(code)
                at_lane = lane == jnp.where(valid, z, -1)
                line = target[x, half, pl.ds(row, 1), :]
                seen = observed_ref[1024 * (step - 1) + receiver]
                picked[step - 1, pl.ds(entry, 1), :] = jnp.where(at_lane, line - seen, 0.0)
            return carry

        lax.fori_loop(0, (number + 3) // 4, sample, 0)

    clear(field_a, (4, EXT - 4), range(1, 11))
    clear(field_b, (0, 8), range(12))
    clear(field_b, (8, EXT - 8), (0, 1, 9, 10, 11))
    clear(field_b, (EXT - 8, EXT), range(12))
    wait_all(later)

    def scale(index, carry):
        x = index + HALO
        for half in range(2):
            for tile in range(5):
                rows = pl.ds(TOP + 8 * tile, 8)
                factor = courant[x, half, rows, :]
                field_c[x, half, rows, :] = field_c[x, half, rows, :] * factor
                field_a[x, half, rows, :] = stage[index, half, pl.ds(8 * tile, 8), :] * factor
        return carry

    lax.fori_loop(0, OWN, scale, 0)
    chain = ((field_c, field_a, field_a), (field_a, field_c, field_c), (field_c, field_a, field_b))
    for step in range(ITERS, 1, -1):
        newer, older, target = chain[ITERS - step]

        def emit(x, half, row, centre, total):
            rows = pl.ds(row, 8)
            target[x, half, rows, :] = (
                centre + centre - older[x, half, rows, :] + courant[x, half, rows, :] * total
            )

        stencil_pass(newer, z_ref, matrices, step, emit)

        def inject(entry, carry):
            _, x, row, half, _ = unpack(own_ref[entry])
            rows = pl.ds(row, 1)
            target[x, half, rows, :] += (
                courant[x, half, rows, :] * picked[step - 1, pl.ds(entry, 1), :]
            )
            return carry

        lax.fori_loop(0, number, inject, 0)

    def prepare(entry, carry):
        _, x, row, half, _ = unpack(own_ref[entry])
        rows = pl.ds(row, 1)
        picked[0, pl.ds(entry, 1), :] = (
            picked[0, pl.ds(entry, 1), :]
            * courant[x, half, rows, :]
            * term_a[x - 4, half, pl.ds(row - 8, 1), :]
        )
        return carry

    lax.fori_loop(0, number, prepare, 0)

    def emit(x, half, row, centre, total):
        rows, place = pl.ds(row, 8), pl.ds(row - 8, 8)
        value = centre + centre - field_c[x, half, rows, :] + courant[x, half, rows, :] * total
        term_a[x - 4, half, place, :] = value * term_a[x - 4, half, place, :]

    stencil_pass(field_b, z_ref, matrices, 1, emit)

    def finish(entry, carry):
        _, x, row, half, _ = unpack(own_ref[entry])
        term_a[x - 4, half, pl.ds(row - 8, 1), :] += picked[0, pl.ds(entry, 1), :]
        return carry

    lax.fori_loop(0, number, finish, 0)

    coarse = planes
    clear(coarse, (0, 20), range(9))
    limit_x = 79 - (base_ref[0] // 4 - 4)

    def image(a, carry):
        higher = jnp.clip(limit_x, 0, a + 1)
        for half in range(2):
            for tile in range(9):
                rows, place = pl.ds(8 + 8 * tile, 8), pl.ds(8 * tile, 8)
                low, high = None, None
                for g in range(4):
                    x = 4 + 4 * a + g
                    total = term_a[x - 4, half, place, :] + (
                        field_b[x, half, rows, :]
                        * term_b[jnp.clip(x - 8, 0, 63), half, place, :]
                    )
                    if 0 < tile < 8:
                        total = total + (
                            field_c[x, half, rows, :]
                            * term_c[jnp.clip(x - 12, 0, 55), half, place, :]
                        )
                        total = total + (
                            field_a[x, half, rows, :]
                            * term_d[jnp.clip(x - 16, 0, 47), half, place, :]
                        )
                    total = total * lax.rsqrt(jnp.maximum(courant[x, half, rows, :], 1e-9))
                    weight = 0.25 * g
                    low = total if low is None else low + (1.0 - weight) * total
                    if g:
                        part = weight * total
                        high = part if high is None else high + part
                coarse[a, half, place, :] += low
                coarse[higher, half, place, :] += high
        return carry

    lax.fori_loop(0, 18, image, 0)
    row = lax.broadcasted_iota(jnp.int32, (24, WIDE), 0)
    fine = lax.broadcasted_iota(jnp.int32, (24, WIDE), 1)
    limit_y = 159 - (base_ref[1] // 4 - 4)
    weight_y = hat(fine, row, fine // 4, limit_y, quarter(fine))
    column = lax.broadcasted_iota(jnp.int32, (64, 256), 0)
    fine = lax.broadcasted_iota(jnp.int32, (64, 256), 1)
    weight_z = hat(fine, column, fine // 4, 63, quarter(fine))
    parts = [jnp.zeros((24, 256), jnp.float32)]
    for a in range(19):
        plane = jnp.concatenate(
            [coarse[a, half, pl.ds(0, WIDE), :] for half in range(2)], axis=1
        )
        parts.append(
            jnp.dot(weight_y, plane, precision=EXACT, preferred_element_type=jnp.float32)
        )
    parts.append(jnp.zeros((32, 256), jnp.float32))
    result = (0.125 * 2.0 * SCALE**0.5) * lax.dot_general(
        weight_z, jnp.concatenate(parts, axis=0), (((1,), (1,)), ((), ())),
        precision=EXACT, preferred_element_type=jnp.float32,
    )
    out_ref[...] = jnp.zeros(out_ref.shape, jnp.float32)
    index = base_ref[0] // OWN
    for piece in range(4):
        owner = 2 * index - 1 + piece

        @pl.when((owner >= 0) & (owner < 16))
        def _():
            moved = pltpu.roll(result, (512 - 120 * piece) % 512, 1) if piece else result
            for i in range(8):
                out_ref[i, owner] = moved[8 * i : 8 * i + 8, :LANES]


def gather_kernel(base_ref, parts_ref, out_ref):
    wide = lax.broadcasted_iota(jnp.int32, (8, 256), 1)
    index = base_ref[1] // OWN
    one = index // 2
    other = jnp.where(index % 2 == 0, one - 1, one + 1)
    valid = (other >= 0) & (other < 8)
    other = jnp.clip(other, 0, 7)
    sums = [jnp.zeros((8, 256), jnp.float32) for _ in range(5)]
    for j in range(16):
        tile = parts_ref[one, j] + jnp.where(valid, parts_ref[other, j], 0.0)
        tile = jnp.concatenate([tile, jnp.zeros((8, LANES), jnp.float32)], axis=1)
        inside = (wide >= 10 * j - 4) & (wide < 10 * j + 15)
        for r in range(5):
            moved = pltpu.roll(tile, (10 * j - 4 - 24 * r) % 256, 1)
            sums[r] = sums[r] + jnp.where(inside, moved, 0.0)
    for r in range(5):
        out_ref[r] = sums[r]


def face_kernel(now, before, *refs):
    outs, stages, sem = refs[:4], refs[4:8], refs[8]
    pairs = []
    for side, (first, second, strip_first) in enumerate(((20, 24, 16), (0, 0, 0))):
        face, strip = stages[side], stages[2 + side]
        pairs += [
            (now.at[pl.ds(first, 20)], face.at[pl.ds(0, 20)]),
            (before.at[pl.ds(second, 16)], face.at[pl.ds(20, 16)]),
            (now.at[:, pl.ds(strip_first, 24)], strip.at[:, pl.ds(0, 24)]),
            (before.at[:, pl.ds(second, 16)], strip.at[:, pl.ds(24, 16)]),
        ]
    wait_all(start_all(pairs, sem))
    wait_all(start_all(list(zip(stages, outs)), sem))


def corner_kernel(x_low, x_high, up, down, stage_up, stage_down, sem):
    pairs = []
    for target, near, far in ((stage_up, 32, 24), (stage_down, 0, 8)):
        for piece, start, places in ((x_low, 0, (4, 12, 24, 32)), (x_high, 40, (0, 0, 20, 20))):
            place = start
            for plane, row, count in zip(places, (near, far, near, far), (16, 8, 12, 4)):
                pairs.append((
                    piece.at[pl.ds(plane, count), pl.ds(row, 8)],
                    target.at[pl.ds(place, count)],
                ))
                place += count
    wait_all(start_all(pairs, sem))
    wait_all(start_all([(stage_up, up), (stage_down, down)], sem))


def gate_kernel(*refs):
    pass


def gate(arrays, tokens):
    return pl.pallas_call(
        gate_kernel,
        out_shape=tuple(jax.ShapeDtypeStruct(a.shape, a.dtype) for a in arrays),
        in_specs=[spec(HBM)] * len(arrays) + [spec(pl.ANY)] * len(tokens),
        out_specs=(spec(HBM),) * len(arrays),
        input_output_aliases={i: i for i in range(len(arrays))},
        cost_estimate=cost(1000, 1000),
    )(*arrays, *tokens)


def shifts(axis, block_up, block_down):
    count = lax.axis_size(axis)
    up = [(i, i + 1) for i in range(count - 1)]
    down = [(i + 1, i) for i in range(count - 1)]
    return lax.ppermute(block_up, axis, up), lax.ppermute(block_down, axis, down)


def staged(kernel, shapes, operands, size):
    shapes = tuple(jax.ShapeDtypeStruct(shape, jnp.float32) for shape in shapes)
    return pl.pallas_call(
        kernel,
        out_shape=shapes,
        in_specs=[spec(HBM)] * len(operands),
        out_specs=(spec(HBM),) * len(shapes),
        scratch_shapes=[VMEM(shape.shape, shape.dtype) for shape in shapes]
        + [pltpu.SemaphoreType.DMA],
        cost_estimate=cost(1000, size),
    )(*operands)


def per_device(
    velocity, forward_now, forward_before, adjoint_now, adjoint_after,
    source_cells, receiver_cells, wavelet, observed,
):
    index_x = lax.axis_index("gx")
    index_y = lax.axis_index("gy")
    base = jnp.stack([index_x * OWN, index_y * OWN]).astype(jnp.int32)
    everywhere = ("gx", "gy")
    buffer = jax.ShapeDtypeStruct((8, 16, 8, LANES), jnp.float32)

    turned = jnp.pad(velocity.transpose(0, 2, 1), ((0, 0), (0, 0), (4, 92)))
    windows = pl.pallas_call(
        model_pack_kernel,
        out_shape=buffer,
        in_specs=[spec(VMEM)],
        out_specs=spec(VMEM),
        cost_estimate=cost(100_000, 600_000),
    )(turned)
    model = lax.all_to_all(windows.reshape(128, 8, LANES), everywhere, 0, 0, tiled=True)
    model = model.reshape(8, 16, 8, LANES)

    own_list, counts = pl.pallas_call(
        list_kernel,
        out_shape=(
            jax.ShapeDtypeStruct((1024,), jnp.int32),
            jax.ShapeDtypeStruct((1,), jnp.int32),
        ),
        in_specs=[spec(SMEM)],
        out_specs=(spec(SMEM),) * 2,
        cost_estimate=cost(10_000_000, 20_000_000),
    )(receiver_codes(receiver_cells, base))

    faces = staged(
        face_kernel, ((36, OWN, 256),) * 2 + ((OWN, 40, 256),) * 2,
        (forward_now, forward_before), 9_000_000,
    )
    x_up, x_down, y_up, y_down = gate(faces, (windows,))
    x_low, x_high = shifts("gx", x_up, x_down)
    y_low, y_high = shifts("gy", y_up, y_down)

    plane_shape = (20, 2, ROWS, LANES)
    planes = pl.pallas_call(
        model_kernel,
        out_shape=jax.ShapeDtypeStruct(plane_shape, jnp.float32),
        in_specs=[spec(SMEM), spec(VMEM)],
        out_specs=spec(HBM),
        scratch_shapes=[VMEM(plane_shape, jnp.float32), pltpu.SemaphoreType.DMA],
        compiler_params=params(32),
        cost_estimate=cost(10_000_000, 10_000_000),
    )(base, model)

    corners = staged(corner_kernel, ((80, 8, 256),) * 2, (x_low, x_high), 2_000_000)
    c_low, c_high = shifts("gy", *corners)

    field = VMEM((EXT, 2, ROWS, LANES), jnp.float32)
    parts = pl.pallas_call(
        propagate_kernel,
        out_shape=buffer,
        in_specs=[spec(SMEM)] * 6 + [spec(VMEM)] * 4 + [spec(HBM)] * 8 + [spec(pl.ANY)] * 3,
        out_specs=spec(VMEM),
        scratch_shapes=[
            field, field, field,
            VMEM((OWN, 2, OWN, LANES), jnp.float32),
            field,
            *(VMEM((EXT - 8 * s, 2, WIDE, LANES), jnp.float32) for s in range(1, 5)),
            VMEM(plane_shape, jnp.float32),
            VMEM((ITERS, 1024, LANES), jnp.float32),
            pltpu.SemaphoreType.DMA((4,)),
        ],
        compiler_params=params(60),
        cost_estimate=cost(200_000_000, 30_000_000),
    )(
        base, source_cells.reshape(-1), wavelet.reshape(-1), own_list, counts,
        observed.reshape(-1), z_matrix(), y_matrix(80, 96), y_matrix(64, 80), y_matrix(48, 64),
        forward_now, forward_before, adjoint_now, adjoint_after,
        x_low, x_high, y_low, y_high, c_low, c_high, planes,
    )

    parts = lax.all_to_all(parts.reshape(128, 8, LANES), everywhere, 0, 0, tiled=True)
    grid = pl.pallas_call(
        gather_kernel,
        out_shape=jax.ShapeDtypeStruct((5, 8, 256), jnp.float32),
        in_specs=[spec(SMEM), spec(VMEM)],
        out_specs=spec(VMEM),
        cost_estimate=cost(100_000, 600_000),
    )(base, parts.reshape(8, 16, 8, LANES))
    return grid[:, :, :160].transpose(0, 2, 1)


def solution(mesh):
    return jax.shard_map(
        per_device,
        mesh=mesh,
        in_specs=(
            P("gy", None, "gx"),
            P("gx", "gy", None),
            P("gx", "gy", None),
            P("gx", "gy", None),
            P("gx", "gy", None),
            P(),
            P(),
            P(),
            P(),
        ),
        out_specs=P("gy", None, "gx"),
        check_vma=False,
    )
```

```python
import jax
import jax.numpy as jnp
from jax import lax
from jax.experimental import pallas as pl
from jax.experimental.pallas import tpu as pltpu
from jax.sharding import PartitionSpec as P

ITERS = 4
OWN = 40
HALO = 20
SPLIT = 40
EXT = OWN + 2 * HALO
TOP = 24
ROWS = 96
WIDE = 72
LANES = 128
CENTRE = -43050.0
RING = (8064.0, -1008.0, 128.0, -9.0)
SCALE = 0.01 / 5040.0
SMEM = pltpu.SMEM
VMEM = pltpu.VMEM
HBM = pltpu.HBM


def params(mib):
    return pltpu.CompilerParams(vmem_limit_bytes=mib * 1024 * 1024)


def cost(flops, size):
    return pl.CostEstimate(flops=flops, bytes_accessed=size, transcendentals=0)


def spec(space):
    return pl.BlockSpec(memory_space=space)


def z_matrix():
    row = lax.broadcasted_iota(jnp.int32, (256, 256), 0)
    column = lax.broadcasted_iota(jnp.int32, (256, 256), 1)
    distance = jnp.abs(row - column)
    result = jnp.zeros((256, 256), jnp.float32)
    for reach, value in enumerate(RING):
        result = jnp.where(distance == reach + 1, value, result)
    return result.astype(jnp.bfloat16)


def y_matrix(rows, window):
    row = lax.broadcasted_iota(jnp.int32, (rows, 2 * window), 0)
    column = lax.broadcasted_iota(jnp.int32, (rows, 2 * window), 1) % window
    distance = jnp.abs(column - 8 - row)
    result = jnp.zeros((rows, 2 * window), jnp.float32)
    for reach, value in enumerate(RING):
        result = jnp.where(distance == reach + 1, value, result)
    return result.astype(jnp.bfloat16)


def hat(fine, coarse, lower, limit, fraction):
    higher = jnp.minimum(lower + 1, limit)
    first = jnp.where(coarse == lower, 1.0 - fraction, 0.0)
    second = jnp.where(coarse == higher, fraction, 0.0)
    return first + second


def thirds(data):
    upper = data.astype(jnp.bfloat16)
    rest = data - upper.astype(jnp.float32)
    middle = rest.astype(jnp.bfloat16)
    return upper, middle, (rest - middle.astype(jnp.float32)).astype(jnp.bfloat16)


def exact_dot(weight, data):
    return sum(
        jnp.dot(weight, part, preferred_element_type=jnp.float32) for part in thirds(data)
    )


def quarter(fine):
    return (fine & 3).astype(jnp.float32) * 0.25


def start_all(pairs, sem):
    started = [pltpu.make_async_copy(a, b, sem) for a, b in pairs]
    for copy in started:
        copy.start()
    return started


def wait_all(started):
    for copy in started:
        copy.wait()


def list_kernel(code_ref, own_ref, count_ref):
    def body(receiver, own):
        code = code_ref[receiver]
        own_ref[own] = code
        return own + lax.shift_right_logical(code, 31)

    count_ref[0] = lax.fori_loop(0, 1024, body, 0, unroll=16)


def receiver_codes(cells, base):
    x = cells[0] - base[0]
    y = cells[1] - base[1]
    own = (x >= 0) & (x < OWN) & (y >= 0) & (y < OWN)
    code = jnp.arange(1024, dtype=jnp.int32) | (cells[2] << 10)
    code = code | ((y & 63) << 18) | ((x & 63) << 24)
    return code | (own.astype(jnp.int32) << 31)


def unpack(code):
    receiver = code & 1023
    z = (code >> 10) & 255
    y = (code >> 18) & 63
    x = (code >> 24) & 63
    return receiver, x + HALO, y + TOP, z // LANES, z & (LANES - 1)


def model_pack_kernel(velocity_ref, out_ref):
    lane = lax.broadcasted_iota(jnp.int32, (8, LANES), 1)
    blocks = [velocity_ref[a] for a in range(5)]
    for j in range(16):
        tile = jnp.zeros((8, LANES), jnp.float32)
        for a in range(5):
            moved = pltpu.roll(blocks[a], (24 * a - 10 * j) % 256, 1)[:, :LANES]
            tile = jnp.where((lane >= 24 * a) & (lane < 24 * a + 24), moved, tile)
        for i in range(8):
            out_ref[i, j] = tile


def model_kernel(base_ref, model_ref, plane_out, plane_ref, sem):
    row = lax.broadcasted_iota(jnp.int32, (64, 256), 0)
    column = lax.broadcasted_iota(jnp.int32, (64, 256), 1)
    weight_z = hat(column, row, column // 4, 63, quarter(column)).astype(jnp.bfloat16)
    fine = lax.broadcasted_iota(jnp.int32, (ROWS, 24), 0)
    coarse = lax.broadcasted_iota(jnp.int32, (ROWS, 24), 1)
    limit_y = 159 - (base_ref[1] // 4 - 4)
    weight_y = hat(fine, coarse, fine // 4 - 2, limit_y, quarter(fine))
    place = fine + (base_ref[1] - TOP)
    weight_y = jnp.where((place >= 0) & (place < 640), weight_y, 0.0).astype(jnp.bfloat16)
    first = 2 * (base_ref[0] // OWN) - 1
    for r in range(4):
        owner = jnp.clip(first + r, 0, 15)
        block = jnp.concatenate([model_ref[i, owner] for i in range(8)], axis=0)
        stacked = jnp.concatenate(thirds(block.T), axis=0)
        deep = jnp.dot(stacked, weight_z, preferred_element_type=jnp.float32)
        deep = deep[:LANES] + deep[LANES : 2 * LANES] + deep[2 * LANES :]
        for a in range(5):
            plane = exact_dot(weight_y, deep[24 * a : 24 * a + 24])
            plane_ref[5 * r + a, 0] = plane[:, :LANES]
            plane_ref[5 * r + a, 1] = plane[:, LANES:]
    wait_all(start_all([(plane_ref, plane_out)], sem))


def fill_courant(base_ref, plane_ref, courant_ref):
    limit_x = 79 - (base_ref[0] // 4 - 5)

    def group(a, carry):
        higher = jnp.minimum(a + 1, limit_x)
        start = base_ref[0] - HALO + 4 * a
        inside = ((start >= 0) & (start < 320)).astype(jnp.float32) * SCALE
        for half in range(2):
            for tile in range(1, 10):
                rows = pl.ds(8 * tile, 8)
                low = plane_ref[a, half, rows, :]
                high = plane_ref[higher, half, rows, :]
                for step in range(4):
                    speed = low * (1.0 - 0.25 * step) + high * (0.25 * step)
                    courant_ref[4 * a + step, half, rows, :] = speed * speed * inside
        return carry

    lax.fori_loop(1, 19, group, 0)


def clear(ref, planes, tiles):
    def body(x, carry):
        for half in range(2):
            for tile in tiles:
                ref[x, half, pl.ds(8 * tile, 8), :] = jnp.zeros((8, LANES), jnp.float32)
        return carry

    lax.fori_loop(planes[0], planes[1], body, 0)


def clear_edges(ref):
    outer = (0, 1, 2, 8, 9, 10, 11)
    clear(ref, (0, HALO), outer)
    clear(ref, (HALO, HALO + OWN), (0, 10, 11))
    clear(ref, (HALO + OWN, EXT), outer)


def copies(now, before, pieces, ext_now, ext_before):
    x_low, x_high, y_low, y_high, c_low, c_high = pieces
    early, late = [], []
    for half in range(2):
        lanes = pl.ds(half * LANES, LANES)

        def add(source, plane, count, row, rows, target, to_plane, to_row):
            (early if to_plane < SPLIT else late).append((
                source.at[pl.ds(plane, count), pl.ds(row, rows), lanes],
                target.at[pl.ds(to_plane, count), half, pl.ds(to_row, rows), :],
            ))

        for plane in (0, SPLIT - HALO):
            place = plane + HALO
            add(now, plane, 20, 0, OWN, ext_now, place, TOP)
            add(before, plane, 20, 0, OWN, ext_before, place, TOP)
            for source, first, second in ((y_low, 0, 8), (y_high, 64, 64)):
                add(source, plane, 20, 0, 24, ext_now, place, first)
                add(source, plane, 20, 24, 16, ext_before, place, second)
        for source, first, second in ((x_low, 0, 4), (x_high, 60, 60)):
            add(source, 0, 20, 0, OWN, ext_now, first, TOP)
            add(source, 20, 16, 0, OWN, ext_before, second, TOP)
        for piece, near, far in ((c_low, 16, 8), (c_high, 64, 72)):
            for side, places in ((0, (4, 12, 8, 16)), (40, (60, 60, 60, 60))):
                add(piece, side, 16, 0, 8, ext_now, places[0], near)
                add(piece, side + 16, 8, 0, 8, ext_now, places[1], far)
                add(piece, side + 24, 12, 0, 8, ext_before, places[2], near)
                add(piece, side + 36, 4, 0, 8, ext_before, places[3], far)
    return early, late


def stencil_pass(source, z_ref, y_refs, step, emit, wait_late=None):
    first = 4 * step
    top = 4 + 4 * step
    span = EXT - 8 * step
    tiles = span // 8
    keep = -(-(8 + span) // 16) * 16
    y_ref, window_rows = ((y_refs[0], 96), (y_refs[1], 80), (y_refs[1], 80), (y_refs[2], 64))[
        step - 1
    ]

    def multiply(x):
        parts = []
        kept = {}
        for g in range(8):
            plane = jnp.concatenate(
                [source[x + g, half, pl.ds(top - 8, window_rows), :] for half in range(2)], axis=1
            )
            upper = plane.astype(jnp.bfloat16)
            lower = (plane - upper.astype(jnp.float32)).astype(jnp.bfloat16)
            parts.append((upper, lower))
        along_z = []
        for pair in (parts[:2], parts[2:4], parts[4:6], parts[6:]):
            stacked = jnp.concatenate(
                [part[side][:keep] for side in range(2) for part in pair], axis=0
            )
            both = jnp.dot(stacked, z_ref[...], preferred_element_type=jnp.float32)
            along_z.append(both[: 2 * keep] + both[2 * keep :])
        for g in range(8):
            along_y = jnp.dot(
                y_ref[...], jnp.concatenate(parts[g], axis=0), preferred_element_type=jnp.float32
            )
            for tile in range(tiles):
                start = (g % 2) * keep + 8 + 8 * tile
                total = along_z[g // 2][start : start + 8] + along_y[8 * tile : 8 * tile + 8]
                for half in range(2):
                    kept[g, tile, half] = total[:, half * LANES : (half + 1) * LANES]
        return kept

    def group(index, carry):
        if wait_late is not None:
            pl.when(index == (SPLIT - 16) // 8)(wait_late)
        x = first + 8 * index
        kept = multiply(x)
        for tile in range(tiles):
            for half in range(2):
                row = top + 8 * tile
                for g in range(8):
                    window = [source[x + g - 4 + j, half, pl.ds(row, 8), :] for j in range(9)]
                    total = CENTRE * window[4]
                    for reach in range(1, 5):
                        total = total + RING[reach - 1] * (window[4 + reach] + window[4 - reach])
                    total = total + kept[g, tile, half]
                    emit(x + g, half, row, window[4], total)
        return carry

    lax.fori_loop(0, span // 8, group, 0)


def propagate_kernel(
    base_ref, source_ref, wavelet_ref, own_ref, count_ref, observed_ref,
    z_ref, y_ref_a, y_ref_b, y_ref_c,
    now, before, adjoint_now, adjoint_after, *refs,
):
    pieces, refs = refs[:6], refs[6:]
    (
        plane_in, out_ref,
        field_a, field_b, field_c, stage, courant, term_a, term_b, term_c, term_d,
        planes, picked, sems,
    ) = refs
    terms = (term_a, term_b, term_c, term_d)
    matrices = (y_ref_a, y_ref_b, y_ref_c)
    first = start_all([(plane_in, planes)], sems.at[0])
    clear_edges(field_a)
    clear_edges(field_b)
    early, late = copies(now, before, pieces, field_b, field_a)
    early = start_all(early, sems.at[1])
    late = start_all(late, sems.at[2])
    clear(field_c, (0, EXT), range(12))
    own = pl.ds(HALO, OWN)
    later = []
    for half in range(2):
        lanes = pl.ds(half * LANES, LANES)
        later += [
            (adjoint_now.at[:, :, lanes], field_c.at[own, half, pl.ds(TOP, OWN), :]),
            (adjoint_after.at[:, :, lanes], stage.at[:, half]),
        ]
    later = start_all(later, sems.at[3])
    clear(term_b, (0, 64), (0, 8))
    clear(term_d, (0, 48), (1, 7))
    wait_all(first)
    fill_courant(base_ref, planes, courant)
    wait_all(early)
    lane = lax.broadcasted_iota(jnp.int32, (1, LANES), 1)
    number = count_ref[0]

    for step in range(1, ITERS + 1):
        target, newer = (field_a, field_b) if step % 2 else (field_b, field_a)
        term = terms[step - 1]
        origin = 4 * step
        span = EXT - 8 * step

        def emit(x, half, row, centre, total):
            rows = pl.ds(row, 8)
            term[x - origin, half, pl.ds(row - 8, 8), :] = total
            target[x, half, rows, :] = (
                centre + centre - target[x, half, rows, :] + courant[x, half, rows, :] * total
            )

        stencil_pass(
            newer, z_ref, matrices, step, emit,
            (lambda: wait_all(late)) if step == 1 else None,
        )
        for source in range(4):
            x = source_ref[source] - (base_ref[0] - HALO)
            row = source_ref[4 + source] - (base_ref[1] - TOP)
            z = source_ref[8 + source]
            inside_x = (x >= origin) & (x < origin + span)
            inside_y = (row >= origin + 4) & (row < origin + 4 + span)

            @pl.when(inside_x & inside_y)
            def _():
                half = z // LANES
                added = jnp.where(
                    lane == (z & (LANES - 1)), wavelet_ref[4 * (step - 1) + source], 0.0
                )
                target[x, half, pl.ds(row, 1), :] += added
                term[x - origin, half, pl.ds(row - 8, 1), :] += (
                    added / courant[x, half, pl.ds(row, 1), :]
                )

        def sample(index, carry):
            for j in range(4):
                entry = 4 * index + j
                valid = entry < number
                code = jnp.where(valid, own_ref[jnp.minimum(entry, 1023)], 0)
                receiver, x, row, half, z = unpack(code)
                at_lane = lane == jnp.where(valid, z, -1)
                line = target[x, half, pl.ds(row, 1), :]
                seen = observed_ref[1024 * (step - 1) + receiver]
                picked[step - 1, pl.ds(entry, 1), :] = jnp.where(at_lane, line - seen, 0.0)
            return carry

        lax.fori_loop(0, (number + 3) // 4, sample, 0)

    clear(field_a, (4, EXT - 4), range(1, 11))
    clear(field_b, (0, 8), range(12))
    clear(field_b, (8, EXT - 8), (0, 1, 9, 10, 11))
    clear(field_b, (EXT - 8, EXT), range(12))
    wait_all(later)

    def scale(index, carry):
        x = index + HALO
        for half in range(2):
            for tile in range(5):
                rows = pl.ds(TOP + 8 * tile, 8)
                factor = courant[x, half, rows, :]
                field_c[x, half, rows, :] = field_c[x, half, rows, :] * factor
                field_a[x, half, rows, :] = stage[index, half, pl.ds(8 * tile, 8), :] * factor
        return carry

    lax.fori_loop(0, OWN, scale, 0)
    chain = ((field_c, field_a, field_a), (field_a, field_c, field_c), (field_c, field_a, field_b))
    for step in range(ITERS, 1, -1):
        newer, older, target = chain[ITERS - step]

        def emit(x, half, row, centre, total):
            rows = pl.ds(row, 8)
            target[x, half, rows, :] = (
                centre + centre - older[x, half, rows, :] + courant[x, half, rows, :] * total
            )

        stencil_pass(newer, z_ref, matrices, step, emit)

        def inject(entry, carry):
            _, x, row, half, _ = unpack(own_ref[entry])
            rows = pl.ds(row, 1)
            target[x, half, rows, :] += (
                courant[x, half, rows, :] * picked[step - 1, pl.ds(entry, 1), :]
            )
            return carry

        lax.fori_loop(0, number, inject, 0)

    def prepare(entry, carry):
        _, x, row, half, _ = unpack(own_ref[entry])
        rows = pl.ds(row, 1)
        picked[0, pl.ds(entry, 1), :] = (
            picked[0, pl.ds(entry, 1), :]
            * courant[x, half, rows, :]
            * term_a[x - 4, half, pl.ds(row - 8, 1), :]
        )
        return carry

    lax.fori_loop(0, number, prepare, 0)

    def emit(x, half, row, centre, total):
        rows, place = pl.ds(row, 8), pl.ds(row - 8, 8)
        value = centre + centre - field_c[x, half, rows, :] + courant[x, half, rows, :] * total
        term_a[x - 4, half, place, :] = value * term_a[x - 4, half, place, :]

    stencil_pass(field_b, z_ref, matrices, 1, emit)

    def finish(entry, carry):
        _, x, row, half, _ = unpack(own_ref[entry])
        term_a[x - 4, half, pl.ds(row - 8, 1), :] += picked[0, pl.ds(entry, 1), :]
        return carry

    lax.fori_loop(0, number, finish, 0)

    coarse = planes
    clear(coarse, (0, 20), range(9))
    limit_x = 79 - (base_ref[0] // 4 - 4)

    def image(a, carry):
        higher = jnp.clip(limit_x, 0, a + 1)
        for half in range(2):
            for tile in range(9):
                rows, place = pl.ds(8 + 8 * tile, 8), pl.ds(8 * tile, 8)
                low, high = None, None
                for g in range(4):
                    x = 4 + 4 * a + g
                    total = term_a[x - 4, half, place, :] + (
                        field_b[x, half, rows, :]
                        * term_b[jnp.clip(x - 8, 0, 63), half, place, :]
                    )
                    if 0 < tile < 8:
                        total = total + (
                            field_c[x, half, rows, :]
                            * term_c[jnp.clip(x - 12, 0, 55), half, place, :]
                        )
                        total = total + (
                            field_a[x, half, rows, :]
                            * term_d[jnp.clip(x - 16, 0, 47), half, place, :]
                        )
                    total = total * lax.rsqrt(jnp.maximum(courant[x, half, rows, :], 1e-9))
                    weight = 0.25 * g
                    low = total if low is None else low + (1.0 - weight) * total
                    if g:
                        part = weight * total
                        high = part if high is None else high + part
                coarse[a, half, place, :] += low
                coarse[higher, half, place, :] += high
        return carry

    lax.fori_loop(0, 18, image, 0)
    row = lax.broadcasted_iota(jnp.int32, (24, WIDE), 0)
    fine = lax.broadcasted_iota(jnp.int32, (24, WIDE), 1)
    limit_y = 159 - (base_ref[1] // 4 - 4)
    weight_y = hat(fine, row, fine // 4, limit_y, quarter(fine)).astype(jnp.bfloat16)
    column = lax.broadcasted_iota(jnp.int32, (64, 256), 0)
    fine = lax.broadcasted_iota(jnp.int32, (64, 256), 1)
    weight_z = hat(fine, column, fine // 4, 63, quarter(fine)).astype(jnp.bfloat16)
    parts = [jnp.zeros((24, 256), jnp.float32)]
    for a in range(19):
        plane = jnp.concatenate(
            [coarse[a, half, pl.ds(0, WIDE), :] for half in range(2)], axis=1
        )
        parts.append(exact_dot(weight_y, plane))
    parts.append(jnp.zeros((32, 256), jnp.float32))
    result = (0.125 * 2.0 * SCALE**0.5) * sum(
        lax.dot_general(
            weight_z, part, (((1,), (1,)), ((), ())), preferred_element_type=jnp.float32
        )
        for part in thirds(jnp.concatenate(parts, axis=0))
    )
    out_ref[...] = jnp.zeros(out_ref.shape, jnp.float32)
    index = base_ref[0] // OWN
    for piece in range(4):
        owner = 2 * index - 1 + piece

        @pl.when((owner >= 0) & (owner < 16))
        def _():
            moved = pltpu.roll(result, (512 - 120 * piece) % 512, 1) if piece else result
            for i in range(8):
                out_ref[i, owner] = moved[8 * i : 8 * i + 8, :LANES]


def gather_kernel(base_ref, parts_ref, out_ref):
    wide = lax.broadcasted_iota(jnp.int32, (8, 256), 1)
    index = base_ref[1] // OWN
    one = index // 2
    other = jnp.where(index % 2 == 0, one - 1, one + 1)
    valid = (other >= 0) & (other < 8)
    other = jnp.clip(other, 0, 7)
    sums = [jnp.zeros((8, 256), jnp.float32) for _ in range(5)]
    for j in range(16):
        tile = parts_ref[one, j] + jnp.where(valid, parts_ref[other, j], 0.0)
        tile = jnp.concatenate([tile, jnp.zeros((8, LANES), jnp.float32)], axis=1)
        inside = (wide >= 10 * j - 4) & (wide < 10 * j + 15)
        for r in range(5):
            moved = pltpu.roll(tile, (10 * j - 4 - 24 * r) % 256, 1)
            sums[r] = sums[r] + jnp.where(inside, moved, 0.0)
    for r in range(5):
        out_ref[r] = sums[r]


def face_kernel(now, before, *refs):
    outs, stages, sem = refs[:4], refs[4:8], refs[8]
    pairs = []
    for side, (first, second, strip_first) in enumerate(((20, 24, 16), (0, 0, 0))):
        face, strip = stages[side], stages[2 + side]
        pairs += [
            (now.at[pl.ds(first, 20)], face.at[pl.ds(0, 20)]),
            (before.at[pl.ds(second, 16)], face.at[pl.ds(20, 16)]),
            (now.at[:, pl.ds(strip_first, 24)], strip.at[:, pl.ds(0, 24)]),
            (before.at[:, pl.ds(second, 16)], strip.at[:, pl.ds(24, 16)]),
        ]
    wait_all(start_all(pairs, sem))
    wait_all(start_all(list(zip(stages, outs)), sem))


def corner_kernel(x_low, x_high, up, down, stage_up, stage_down, sem):
    pairs = []
    for target, near, far in ((stage_up, 32, 24), (stage_down, 0, 8)):
        for piece, start, places in ((x_low, 0, (4, 12, 24, 32)), (x_high, 40, (0, 0, 20, 20))):
            place = start
            for plane, row, count in zip(places, (near, far, near, far), (16, 8, 12, 4)):
                pairs.append((
                    piece.at[pl.ds(plane, count), pl.ds(row, 8)],
                    target.at[pl.ds(place, count)],
                ))
                place += count
    wait_all(start_all(pairs, sem))
    wait_all(start_all([(stage_up, up), (stage_down, down)], sem))


def gate_kernel(*refs):
    pass


def gate(arrays, tokens):
    return pl.pallas_call(
        gate_kernel,
        out_shape=tuple(jax.ShapeDtypeStruct(a.shape, a.dtype) for a in arrays),
        in_specs=[spec(HBM)] * len(arrays) + [spec(pl.ANY)] * len(tokens),
        out_specs=(spec(HBM),) * len(arrays),
        input_output_aliases={i: i for i in range(len(arrays))},
        cost_estimate=cost(1000, 1000),
    )(*arrays, *tokens)


def shifts(axis, block_up, block_down):
    count = lax.axis_size(axis)
    up = [(i, i + 1) for i in range(count - 1)]
    down = [(i + 1, i) for i in range(count - 1)]
    return lax.ppermute(block_up, axis, up), lax.ppermute(block_down, axis, down)


def staged(kernel, shapes, operands, size):
    shapes = tuple(jax.ShapeDtypeStruct(shape, jnp.float32) for shape in shapes)
    return pl.pallas_call(
        kernel,
        out_shape=shapes,
        in_specs=[spec(HBM)] * len(operands),
        out_specs=(spec(HBM),) * len(shapes),
        scratch_shapes=[VMEM(shape.shape, shape.dtype) for shape in shapes]
        + [pltpu.SemaphoreType.DMA],
        cost_estimate=cost(1000, size),
    )(*operands)


def per_device(
    velocity, forward_now, forward_before, adjoint_now, adjoint_after,
    source_cells, receiver_cells, wavelet, observed,
):
    index_x = lax.axis_index("gx")
    index_y = lax.axis_index("gy")
    base = jnp.stack([index_x * OWN, index_y * OWN]).astype(jnp.int32)
    everywhere = ("gx", "gy")
    buffer = jax.ShapeDtypeStruct((8, 16, 8, LANES), jnp.float32)

    turned = jnp.pad(velocity.transpose(0, 2, 1), ((0, 0), (0, 0), (4, 92)))
    windows = pl.pallas_call(
        model_pack_kernel,
        out_shape=buffer,
        in_specs=[spec(VMEM)],
        out_specs=spec(VMEM),
        cost_estimate=cost(100_000, 600_000),
    )(turned)
    model = lax.all_to_all(windows.reshape(128, 8, LANES), everywhere, 0, 0, tiled=True)
    model = model.reshape(8, 16, 8, LANES)

    own_list, counts = pl.pallas_call(
        list_kernel,
        out_shape=(
            jax.ShapeDtypeStruct((1024,), jnp.int32),
            jax.ShapeDtypeStruct((1,), jnp.int32),
        ),
        in_specs=[spec(SMEM)],
        out_specs=(spec(SMEM),) * 2,
        cost_estimate=cost(10_000_000, 20_000_000),
    )(receiver_codes(receiver_cells, base))

    faces = staged(
        face_kernel, ((36, OWN, 256),) * 2 + ((OWN, 40, 256),) * 2,
        (forward_now, forward_before), 9_000_000,
    )
    x_up, x_down, y_up, y_down = gate(faces, (windows,))
    x_low, x_high = shifts("gx", x_up, x_down)
    y_low, y_high = shifts("gy", y_up, y_down)

    plane_shape = (20, 2, ROWS, LANES)
    planes = pl.pallas_call(
        model_kernel,
        out_shape=jax.ShapeDtypeStruct(plane_shape, jnp.float32),
        in_specs=[spec(SMEM), spec(VMEM)],
        out_specs=spec(HBM),
        scratch_shapes=[VMEM(plane_shape, jnp.float32), pltpu.SemaphoreType.DMA],
        compiler_params=params(32),
        cost_estimate=cost(10_000_000, 10_000_000),
    )(base, model)

    corners = staged(corner_kernel, ((80, 8, 256),) * 2, (x_low, x_high), 2_000_000)
    c_low, c_high = shifts("gy", *corners)

    field = VMEM((EXT, 2, ROWS, LANES), jnp.float32)
    parts = pl.pallas_call(
        propagate_kernel,
        out_shape=buffer,
        in_specs=[spec(SMEM)] * 6 + [spec(VMEM)] * 4 + [spec(HBM)] * 8 + [spec(pl.ANY)] * 3,
        out_specs=spec(VMEM),
        scratch_shapes=[
            field, field, field,
            VMEM((OWN, 2, OWN, LANES), jnp.float32),
            field,
            *(VMEM((EXT - 8 * s, 2, WIDE, LANES), jnp.float32) for s in range(1, 5)),
            VMEM(plane_shape, jnp.float32),
            VMEM((ITERS, 1024, LANES), jnp.float32),
            pltpu.SemaphoreType.DMA((4,)),
        ],
        compiler_params=params(60),
        cost_estimate=cost(200_000_000, 30_000_000),
    )(
        base, source_cells.reshape(-1), wavelet.reshape(-1), own_list, counts,
        observed.reshape(-1), z_matrix(), y_matrix(80, 96), y_matrix(64, 80), y_matrix(48, 64),
        forward_now, forward_before, adjoint_now, adjoint_after,
        x_low, x_high, y_low, y_high, c_low, c_high, planes,
    )

    parts = lax.all_to_all(parts.reshape(128, 8, LANES), everywhere, 0, 0, tiled=True)
    grid = pl.pallas_call(
        gather_kernel,
        out_shape=jax.ShapeDtypeStruct((5, 8, 256), jnp.float32),
        in_specs=[spec(SMEM), spec(VMEM)],
        out_specs=spec(VMEM),
        cost_estimate=cost(100_000, 600_000),
    )(base, parts.reshape(8, 16, 8, LANES))
    return grid[:, :, :160].transpose(0, 2, 1)


def solution(mesh):
    return jax.shard_map(
        per_device,
        mesh=mesh,
        in_specs=(
            P("gy", None, "gx"),
            P("gx", "gy", None),
            P("gx", "gy", None),
            P("gx", "gy", None),
            P("gx", "gy", None),
            P(),
            P(),
            P(),
            P(),
        ),
        out_specs=P("gy", None, "gx"),
        check_vma=False,
    )
```

```python
import jax
import jax.numpy as jnp
from jax import lax
from jax.experimental import pallas as pl
from jax.experimental.pallas import tpu as pltpu
from jax.sharding import PartitionSpec as P

ITERS = 4
OWN = 40
HALO = 20
SPLIT = 40
EXT = OWN + 2 * HALO
TOP = 24
ROWS = 96
WIDE = 72
LANES = 128
CENTRE = -43050.0
RING = (8064.0, -1008.0, 128.0, -9.0)
SCALE = 0.01 / 5040.0
SMEM = pltpu.SMEM
VMEM = pltpu.VMEM
HBM = pltpu.HBM


def params(mib):
    return pltpu.CompilerParams(vmem_limit_bytes=mib * 1024 * 1024)


def cost(flops, size):
    return pl.CostEstimate(flops=flops, bytes_accessed=size, transcendentals=0)


def spec(space):
    return pl.BlockSpec(memory_space=space)


def z_matrix():
    row = lax.broadcasted_iota(jnp.int32, (256, 256), 0)
    column = lax.broadcasted_iota(jnp.int32, (256, 256), 1)
    distance = jnp.abs(row - column)
    result = jnp.zeros((256, 256), jnp.float32)
    for reach, value in enumerate(RING):
        result = jnp.where(distance == reach + 1, value, result)
    return result.astype(jnp.bfloat16)


def y_matrix(rows, window):
    row = lax.broadcasted_iota(jnp.int32, (rows, 2 * window), 0)
    column = lax.broadcasted_iota(jnp.int32, (rows, 2 * window), 1) % window
    distance = jnp.abs(column - 8 - row)
    result = jnp.zeros((rows, 2 * window), jnp.float32)
    for reach, value in enumerate(RING):
        result = jnp.where(distance == reach + 1, value, result)
    return result.astype(jnp.bfloat16)


def hat(fine, coarse, lower, limit, fraction):
    higher = jnp.minimum(lower + 1, limit)
    first = jnp.where(coarse == lower, 1.0 - fraction, 0.0)
    second = jnp.where(coarse == higher, fraction, 0.0)
    return first + second


def thirds(data):
    upper = data.astype(jnp.bfloat16)
    rest = data - upper.astype(jnp.float32)
    middle = rest.astype(jnp.bfloat16)
    return upper, middle, (rest - middle.astype(jnp.float32)).astype(jnp.bfloat16)


def exact_dot(weight, data):
    return sum(
        jnp.dot(weight, part, preferred_element_type=jnp.float32) for part in thirds(data)
    )


def quarter(fine):
    return (fine & 3).astype(jnp.float32) * 0.25


def start_all(pairs, sem):
    started = [pltpu.make_async_copy(a, b, sem) for a, b in pairs]
    for copy in started:
        copy.start()
    return started


def wait_all(started):
    for copy in started:
        copy.wait()


def list_kernel(code_ref, own_ref, count_ref):
    def body(receiver, own):
        code = code_ref[receiver]
        own_ref[own] = code
        return own + lax.shift_right_logical(code, 31)

    count_ref[0] = lax.fori_loop(0, 1024, body, 0, unroll=16)


def receiver_codes(cells, base):
    x = cells[0] - base[0]
    y = cells[1] - base[1]
    own = (x >= 0) & (x < OWN) & (y >= 0) & (y < OWN)
    code = jnp.arange(1024, dtype=jnp.int32) | (cells[2] << 10)
    code = code | ((y & 63) << 18) | ((x & 63) << 24)
    return code | (own.astype(jnp.int32) << 31)


def unpack(code):
    receiver = code & 1023
    z = (code >> 10) & 255
    y = (code >> 18) & 63
    x = (code >> 24) & 63
    return receiver, x + HALO, y + TOP, z // LANES, z & (LANES - 1)


def model_pack_kernel(velocity_ref, out_ref, wide_ref):
    wide_ref[...] = jnp.zeros(wide_ref.shape, jnp.float32)
    wide_ref[:, :, pl.ds(0, 160)] = velocity_ref[...]
    lane = lax.broadcasted_iota(jnp.int32, (8, LANES), 1)
    blocks = [wide_ref[a] for a in range(5)]
    for j in range(16):
        tile = jnp.zeros((8, LANES), jnp.float32)
        for a in range(5):
            moved = pltpu.roll(blocks[a], (24 * a - 10 * j + 4) % 256, 1)[:, :LANES]
            tile = jnp.where((lane >= 24 * a) & (lane < 24 * a + 24), moved, tile)
        for i in range(8):
            out_ref[i, j] = tile


def model_kernel(base_ref, model_ref, plane_out, plane_ref, sem):
    row = lax.broadcasted_iota(jnp.int32, (64, 256), 0)
    column = lax.broadcasted_iota(jnp.int32, (64, 256), 1)
    weight_z = hat(column, row, column // 4, 63, quarter(column)).astype(jnp.bfloat16)
    fine = lax.broadcasted_iota(jnp.int32, (ROWS, 24), 0)
    coarse = lax.broadcasted_iota(jnp.int32, (ROWS, 24), 1)
    limit_y = 159 - (base_ref[1] // 4 - 4)
    weight_y = hat(fine, coarse, fine // 4 - 2, limit_y, quarter(fine))
    place = fine + (base_ref[1] - TOP)
    weight_y = jnp.where((place >= 0) & (place < 640), weight_y, 0.0).astype(jnp.bfloat16)
    first = 2 * (base_ref[0] // OWN) - 1
    for r in range(4):
        owner = jnp.clip(first + r, 0, 15)
        block = jnp.concatenate([model_ref[i, owner] for i in range(8)], axis=0)
        stacked = jnp.concatenate(thirds(block.T), axis=0)
        deep = jnp.dot(stacked, weight_z, preferred_element_type=jnp.float32)
        deep = deep[:LANES] + deep[LANES : 2 * LANES] + deep[2 * LANES :]
        for a in range(5):
            plane = exact_dot(weight_y, deep[24 * a : 24 * a + 24])
            plane_ref[5 * r + a, 0] = plane[:, :LANES]
            plane_ref[5 * r + a, 1] = plane[:, LANES:]
    wait_all(start_all([(plane_ref, plane_out)], sem))


def fill_courant(base_ref, plane_ref, courant_ref):
    limit_x = 79 - (base_ref[0] // 4 - 5)

    def group(a, carry):
        higher = jnp.minimum(a + 1, limit_x)
        start = base_ref[0] - HALO + 4 * a
        inside = ((start >= 0) & (start < 320)).astype(jnp.float32) * SCALE
        for half in range(2):
            for tile in range(1, 10):
                rows = pl.ds(8 * tile, 8)
                low = plane_ref[a, half, rows, :]
                high = plane_ref[higher, half, rows, :]
                for step in range(4):
                    speed = low * (1.0 - 0.25 * step) + high * (0.25 * step)
                    courant_ref[4 * a + step, half, rows, :] = speed * speed * inside
        return carry

    lax.fori_loop(1, 19, group, 0)


def clear(ref, planes, tiles):
    def body(x, carry):
        for half in range(2):
            for tile in tiles:
                ref[x, half, pl.ds(8 * tile, 8), :] = jnp.zeros((8, LANES), jnp.float32)
        return carry

    lax.fori_loop(planes[0], planes[1], body, 0)


def clear_edges(ref):
    outer = (0, 1, 2, 8, 9, 10, 11)
    clear(ref, (0, HALO), outer)
    clear(ref, (HALO, HALO + OWN), (0, 10, 11))
    clear(ref, (HALO + OWN, EXT), outer)


def copies(now, before, pieces, ext_now, ext_before):
    x_low, x_high, y_low, y_high, c_low, c_high = pieces
    early, late = [], []
    for half in range(2):
        lanes = pl.ds(half * LANES, LANES)

        def add(source, plane, count, row, rows, target, to_plane, to_row):
            (early if to_plane < SPLIT else late).append((
                source.at[pl.ds(plane, count), pl.ds(row, rows), lanes],
                target.at[pl.ds(to_plane, count), half, pl.ds(to_row, rows), :],
            ))

        for plane in (0, SPLIT - HALO):
            place = plane + HALO
            add(now, plane, 20, 0, OWN, ext_now, place, TOP)
            add(before, plane, 20, 0, OWN, ext_before, place, TOP)
            for source, first, second in ((y_low, 0, 8), (y_high, 64, 64)):
                add(source, plane, 20, 0, 24, ext_now, place, first)
                add(source, plane, 20, 24, 16, ext_before, place, second)
        for source, first, second in ((x_low, 0, 4), (x_high, 60, 60)):
            add(source, 0, 20, 0, OWN, ext_now, first, TOP)
            add(source, 20, 16, 0, OWN, ext_before, second, TOP)
        for piece, near, far in ((c_low, 16, 8), (c_high, 64, 72)):
            for side, places in ((0, (4, 12, 8, 16)), (40, (60, 60, 60, 60))):
                add(piece, side, 16, 0, 8, ext_now, places[0], near)
                add(piece, side + 16, 8, 0, 8, ext_now, places[1], far)
                add(piece, side + 24, 12, 0, 8, ext_before, places[2], near)
                add(piece, side + 36, 4, 0, 8, ext_before, places[3], far)
    return early, late


def stencil_pass(source, z_ref, y_refs, step, emit, wait_late=None):
    first = 4 * step
    top = 4 + 4 * step
    span = EXT - 8 * step
    tiles = span // 8
    keep = -(-(8 + span) // 16) * 16
    y_ref, window_rows = ((y_refs[0], 96), (y_refs[1], 80), (y_refs[1], 80), (y_refs[2], 64))[
        step - 1
    ]

    def multiply(x):
        parts = []
        kept = {}
        for g in range(8):
            plane = jnp.concatenate(
                [source[x + g, half, pl.ds(top - 8, window_rows), :] for half in range(2)], axis=1
            )
            upper = plane.astype(jnp.bfloat16)
            lower = (plane - upper.astype(jnp.float32)).astype(jnp.bfloat16)
            parts.append((upper, lower))
        along_z = []
        for pair in (parts[:2], parts[2:4], parts[4:6], parts[6:]):
            stacked = jnp.concatenate(
                [part[side][:keep] for side in range(2) for part in pair], axis=0
            )
            both = jnp.dot(stacked, z_ref[...], preferred_element_type=jnp.float32)
            along_z.append(both[: 2 * keep] + both[2 * keep :])
        for g in range(8):
            along_y = jnp.dot(
                y_ref[...], jnp.concatenate(parts[g], axis=0), preferred_element_type=jnp.float32
            )
            for tile in range(tiles):
                start = (g % 2) * keep + 8 + 8 * tile
                total = along_z[g // 2][start : start + 8] + along_y[8 * tile : 8 * tile + 8]
                for half in range(2):
                    kept[g, tile, half] = total[:, half * LANES : (half + 1) * LANES]
        return kept

    def group(index, carry):
        if wait_late is not None:
            pl.when(index == (SPLIT - 16) // 8)(wait_late)
        x = first + 8 * index
        kept = multiply(x)
        for tile in range(tiles):
            for half in range(2):
                row = top + 8 * tile
                for g in range(8):
                    window = [source[x + g - 4 + j, half, pl.ds(row, 8), :] for j in range(9)]
                    total = CENTRE * window[4]
                    for reach in range(1, 5):
                        total = total + RING[reach - 1] * (window[4 + reach] + window[4 - reach])
                    total = total + kept[g, tile, half]
                    emit(x + g, half, row, window[4], total)
        return carry

    lax.fori_loop(0, span // 8, group, 0)


def propagate_kernel(
    base_ref, source_ref, wavelet_ref, own_ref, count_ref, observed_ref,
    z_ref, y_ref_a, y_ref_b, y_ref_c,
    now, before, adjoint_now, adjoint_after, *refs,
):
    pieces, refs = refs[:6], refs[6:]
    (
        plane_in, out_ref,
        field_a, field_b, field_c, stage, courant, term_a, term_b, term_c, term_d,
        planes, picked, sems,
    ) = refs
    terms = (term_a, term_b, term_c, term_d)
    matrices = (y_ref_a, y_ref_b, y_ref_c)
    first = start_all([(plane_in, planes)], sems.at[0])
    clear_edges(field_a)
    clear_edges(field_b)
    early, late = copies(now, before, pieces, field_b, field_a)
    early = start_all(early, sems.at[1])
    late = start_all(late, sems.at[2])
    clear(field_c, (0, EXT), range(12))
    own = pl.ds(HALO, OWN)
    later = []
    for half in range(2):
        lanes = pl.ds(half * LANES, LANES)
        later += [
            (adjoint_now.at[:, :, lanes], field_c.at[own, half, pl.ds(TOP, OWN), :]),
            (adjoint_after.at[:, :, lanes], stage.at[:, half]),
        ]
    later = start_all(later, sems.at[3])
    clear(term_b, (0, 64), (0, 8))
    clear(term_d, (0, 48), (1, 7))
    wait_all(first)
    fill_courant(base_ref, planes, courant)
    wait_all(early)
    lane = lax.broadcasted_iota(jnp.int32, (1, LANES), 1)
    number = count_ref[0]

    for step in range(1, ITERS + 1):
        target, newer = (field_a, field_b) if step % 2 else (field_b, field_a)
        term = terms[step - 1]
        origin = 4 * step
        span = EXT - 8 * step

        def emit(x, half, row, centre, total):
            rows = pl.ds(row, 8)
            term[x - origin, half, pl.ds(row - 8, 8), :] = total
            target[x, half, rows, :] = (
                centre + centre - target[x, half, rows, :] + courant[x, half, rows, :] * total
            )

        stencil_pass(
            newer, z_ref, matrices, step, emit,
            (lambda: wait_all(late)) if step == 1 else None,
        )
        for source in range(4):
            x = source_ref[source] - (base_ref[0] - HALO)
            row = source_ref[4 + source] - (base_ref[1] - TOP)
            z = source_ref[8 + source]
            inside_x = (x >= origin) & (x < origin + span)
            inside_y = (row >= origin + 4) & (row < origin + 4 + span)

            @pl.when(inside_x & inside_y)
            def _():
                half = z // LANES
                added = jnp.where(
                    lane == (z & (LANES - 1)), wavelet_ref[4 * (step - 1) + source], 0.0
                )
                target[x, half, pl.ds(row, 1), :] += added
                term[x - origin, half, pl.ds(row - 8, 1), :] += (
                    added / courant[x, half, pl.ds(row, 1), :]
                )

        def sample(index, carry):
            for j in range(4):
                entry = 4 * index + j
                valid = entry < number
                code = jnp.where(valid, own_ref[jnp.minimum(entry, 1023)], 0)
                receiver, x, row, half, z = unpack(code)
                at_lane = lane == jnp.where(valid, z, -1)
                line = target[x, half, pl.ds(row, 1), :]
                seen = observed_ref[1024 * (step - 1) + receiver]
                picked[step - 1, pl.ds(entry, 1), :] = jnp.where(at_lane, line - seen, 0.0)
            return carry

        lax.fori_loop(0, (number + 3) // 4, sample, 0)

    clear(field_a, (4, EXT - 4), range(1, 11))
    clear(field_b, (0, 8), range(12))
    clear(field_b, (8, EXT - 8), (0, 1, 9, 10, 11))
    clear(field_b, (EXT - 8, EXT), range(12))
    wait_all(later)

    def scale(index, carry):
        x = index + HALO
        for half in range(2):
            for tile in range(5):
                rows = pl.ds(TOP + 8 * tile, 8)
                factor = courant[x, half, rows, :]
                field_c[x, half, rows, :] = field_c[x, half, rows, :] * factor
                field_a[x, half, rows, :] = stage[index, half, pl.ds(8 * tile, 8), :] * factor
        return carry

    lax.fori_loop(0, OWN, scale, 0)
    chain = ((field_c, field_a, field_a), (field_a, field_c, field_c), (field_c, field_a, field_b))
    for step in range(ITERS, 1, -1):
        newer, older, target = chain[ITERS - step]

        def emit(x, half, row, centre, total):
            rows = pl.ds(row, 8)
            target[x, half, rows, :] = (
                centre + centre - older[x, half, rows, :] + courant[x, half, rows, :] * total
            )

        stencil_pass(newer, z_ref, matrices, step, emit)

        def inject(entry, carry):
            _, x, row, half, _ = unpack(own_ref[entry])
            rows = pl.ds(row, 1)
            target[x, half, rows, :] += (
                courant[x, half, rows, :] * picked[step - 1, pl.ds(entry, 1), :]
            )
            return carry

        lax.fori_loop(0, number, inject, 0)

    def prepare(entry, carry):
        _, x, row, half, _ = unpack(own_ref[entry])
        rows = pl.ds(row, 1)
        picked[0, pl.ds(entry, 1), :] = (
            picked[0, pl.ds(entry, 1), :]
            * courant[x, half, rows, :]
            * term_a[x - 4, half, pl.ds(row - 8, 1), :]
        )
        return carry

    lax.fori_loop(0, number, prepare, 0)

    def emit(x, half, row, centre, total):
        rows, place = pl.ds(row, 8), pl.ds(row - 8, 8)
        value = centre + centre - field_c[x, half, rows, :] + courant[x, half, rows, :] * total
        term_a[x - 4, half, place, :] = value * term_a[x - 4, half, place, :]

    stencil_pass(field_b, z_ref, matrices, 1, emit)

    def finish(entry, carry):
        _, x, row, half, _ = unpack(own_ref[entry])
        term_a[x - 4, half, pl.ds(row - 8, 1), :] += picked[0, pl.ds(entry, 1), :]
        return carry

    lax.fori_loop(0, number, finish, 0)

    coarse = planes
    clear(coarse, (0, 20), range(9))
    limit_x = 79 - (base_ref[0] // 4 - 4)

    def image(a, carry):
        higher = jnp.clip(limit_x, 0, a + 1)
        for half in range(2):
            for tile in range(9):
                rows, place = pl.ds(8 + 8 * tile, 8), pl.ds(8 * tile, 8)
                low, high = None, None
                for g in range(4):
                    x = 4 + 4 * a + g
                    total = term_a[x - 4, half, place, :] + (
                        field_b[x, half, rows, :]
                        * term_b[jnp.clip(x - 8, 0, 63), half, place, :]
                    )
                    if 0 < tile < 8:
                        total = total + (
                            field_c[x, half, rows, :]
                            * term_c[jnp.clip(x - 12, 0, 55), half, place, :]
                        )
                        total = total + (
                            field_a[x, half, rows, :]
                            * term_d[jnp.clip(x - 16, 0, 47), half, place, :]
                        )
                    total = total * lax.rsqrt(jnp.maximum(courant[x, half, rows, :], 1e-9))
                    weight = 0.25 * g
                    low = total if low is None else low + (1.0 - weight) * total
                    if g:
                        part = weight * total
                        high = part if high is None else high + part
                coarse[a, half, place, :] += low
                coarse[higher, half, place, :] += high
        return carry

    lax.fori_loop(0, 18, image, 0)
    row = lax.broadcasted_iota(jnp.int32, (24, WIDE), 0)
    fine = lax.broadcasted_iota(jnp.int32, (24, WIDE), 1)
    limit_y = 159 - (base_ref[1] // 4 - 4)
    weight_y = hat(fine, row, fine // 4, limit_y, quarter(fine)).astype(jnp.bfloat16)
    column = lax.broadcasted_iota(jnp.int32, (64, 256), 0)
    fine = lax.broadcasted_iota(jnp.int32, (64, 256), 1)
    weight_z = hat(fine, column, fine // 4, 63, quarter(fine)).astype(jnp.bfloat16)
    parts = [jnp.zeros((24, 256), jnp.float32)]
    for a in range(19):
        plane = jnp.concatenate(
            [coarse[a, half, pl.ds(0, WIDE), :] for half in range(2)], axis=1
        )
        parts.append(exact_dot(weight_y, plane))
    parts.append(jnp.zeros((32, 256), jnp.float32))
    result = (0.125 * 2.0 * SCALE**0.5) * sum(
        lax.dot_general(
            weight_z, part, (((1,), (1,)), ((), ())), preferred_element_type=jnp.float32
        )
        for part in thirds(jnp.concatenate(parts, axis=0))
    )
    out_ref[...] = jnp.zeros(out_ref.shape, jnp.float32)
    index = base_ref[0] // OWN
    for piece in range(4):
        owner = 2 * index - 1 + piece

        @pl.when((owner >= 0) & (owner < 16))
        def _():
            moved = pltpu.roll(result, (512 - 120 * piece) % 512, 1) if piece else result
            for i in range(8):
                out_ref[i, owner] = moved[8 * i : 8 * i + 8, :LANES]


def gather_kernel(base_ref, parts_ref, out_ref):
    wide = lax.broadcasted_iota(jnp.int32, (8, 256), 1)
    index = base_ref[1] // OWN
    one = index // 2
    other = jnp.where(index % 2 == 0, one - 1, one + 1)
    valid = (other >= 0) & (other < 8)
    other = jnp.clip(other, 0, 7)
    sums = [jnp.zeros((8, 256), jnp.float32) for _ in range(5)]
    for j in range(16):
        tile = parts_ref[one, j] + jnp.where(valid, parts_ref[other, j], 0.0)
        tile = jnp.concatenate([tile, jnp.zeros((8, LANES), jnp.float32)], axis=1)
        inside = (wide >= 10 * j - 4) & (wide < 10 * j + 15)
        for r in range(5):
            moved = pltpu.roll(tile, (10 * j - 4 - 24 * r) % 256, 1)
            sums[r] = sums[r] + jnp.where(inside, moved, 0.0)
    for r in range(5):
        out_ref[r] = sums[r][:, :160]


def face_kernel(now, before, *refs):
    outs, stages, sem = refs[:4], refs[4:8], refs[8]
    pairs = []
    for side, (first, second, strip_first) in enumerate(((20, 24, 16), (0, 0, 0))):
        face, strip = stages[side], stages[2 + side]
        pairs += [
            (now.at[pl.ds(first, 20)], face.at[pl.ds(0, 20)]),
            (before.at[pl.ds(second, 16)], face.at[pl.ds(20, 16)]),
            (now.at[:, pl.ds(strip_first, 24)], strip.at[:, pl.ds(0, 24)]),
            (before.at[:, pl.ds(second, 16)], strip.at[:, pl.ds(24, 16)]),
        ]
    wait_all(start_all(pairs, sem))
    wait_all(start_all(list(zip(stages, outs)), sem))


def corner_kernel(x_low, x_high, up, down, stage_up, stage_down, sem):
    pairs = []
    for target, near, far in ((stage_up, 32, 24), (stage_down, 0, 8)):
        for piece, start, places in ((x_low, 0, (4, 12, 24, 32)), (x_high, 40, (0, 0, 20, 20))):
            place = start
            for plane, row, count in zip(places, (near, far, near, far), (16, 8, 12, 4)):
                pairs.append((
                    piece.at[pl.ds(plane, count), pl.ds(row, 8)],
                    target.at[pl.ds(place, count)],
                ))
                place += count
    wait_all(start_all(pairs, sem))
    wait_all(start_all([(stage_up, up), (stage_down, down)], sem))


def gate_kernel(*refs):
    pass


def gate(arrays, tokens):
    return pl.pallas_call(
        gate_kernel,
        out_shape=tuple(jax.ShapeDtypeStruct(a.shape, a.dtype) for a in arrays),
        in_specs=[spec(HBM)] * len(arrays) + [spec(pl.ANY)] * len(tokens),
        out_specs=(spec(HBM),) * len(arrays),
        input_output_aliases={i: i for i in range(len(arrays))},
        cost_estimate=cost(1000, 1000),
    )(*arrays, *tokens)


def shifts(axis, block_up, block_down):
    count = lax.axis_size(axis)
    up = [(i, i + 1) for i in range(count - 1)]
    down = [(i + 1, i) for i in range(count - 1)]
    return lax.ppermute(block_up, axis, up), lax.ppermute(block_down, axis, down)


def staged(kernel, shapes, operands, size):
    shapes = tuple(jax.ShapeDtypeStruct(shape, jnp.float32) for shape in shapes)
    return pl.pallas_call(
        kernel,
        out_shape=shapes,
        in_specs=[spec(HBM)] * len(operands),
        out_specs=(spec(HBM),) * len(shapes),
        scratch_shapes=[VMEM(shape.shape, shape.dtype) for shape in shapes]
        + [pltpu.SemaphoreType.DMA],
        cost_estimate=cost(1000, size),
    )(*operands)


def per_device(
    velocity, forward_now, forward_before, adjoint_now, adjoint_after,
    source_cells, receiver_cells, wavelet, observed,
):
    index_x = lax.axis_index("gx")
    index_y = lax.axis_index("gy")
    base = jnp.stack([index_x * OWN, index_y * OWN]).astype(jnp.int32)
    everywhere = ("gx", "gy")
    buffer = jax.ShapeDtypeStruct((8, 16, 8, LANES), jnp.float32)

    turned = velocity.transpose(0, 2, 1)
    windows = pl.pallas_call(
        model_pack_kernel,
        out_shape=buffer,
        in_specs=[spec(VMEM)],
        out_specs=spec(VMEM),
        scratch_shapes=[VMEM((5, 8, 256), jnp.float32)],
        cost_estimate=cost(100_000, 600_000),
    )(turned)
    model = lax.all_to_all(windows.reshape(128, 8, LANES), everywhere, 0, 0, tiled=True)
    model = model.reshape(8, 16, 8, LANES)

    own_list, counts = pl.pallas_call(
        list_kernel,
        out_shape=(
            jax.ShapeDtypeStruct((1024,), jnp.int32),
            jax.ShapeDtypeStruct((1,), jnp.int32),
        ),
        in_specs=[spec(SMEM)],
        out_specs=(spec(SMEM),) * 2,
        cost_estimate=cost(10_000_000, 20_000_000),
    )(receiver_codes(receiver_cells, base))

    faces = staged(
        face_kernel, ((36, OWN, 256),) * 2 + ((OWN, 40, 256),) * 2,
        (forward_now, forward_before), 9_000_000,
    )
    x_up, x_down, y_up, y_down = gate(faces, (windows,))
    x_low, x_high = shifts("gx", x_up, x_down)
    y_low, y_high = shifts("gy", y_up, y_down)

    plane_shape = (20, 2, ROWS, LANES)
    planes = pl.pallas_call(
        model_kernel,
        out_shape=jax.ShapeDtypeStruct(plane_shape, jnp.float32),
        in_specs=[spec(SMEM), spec(VMEM)],
        out_specs=spec(HBM),
        scratch_shapes=[VMEM(plane_shape, jnp.float32), pltpu.SemaphoreType.DMA],
        compiler_params=params(32),
        cost_estimate=cost(10_000_000, 10_000_000),
    )(base, model)

    corners = staged(corner_kernel, ((80, 8, 256),) * 2, (x_low, x_high), 2_000_000)
    c_low, c_high = shifts("gy", *corners)

    field = VMEM((EXT, 2, ROWS, LANES), jnp.float32)
    parts = pl.pallas_call(
        propagate_kernel,
        out_shape=buffer,
        in_specs=[spec(SMEM)] * 6 + [spec(VMEM)] * 4 + [spec(HBM)] * 8 + [spec(pl.ANY)] * 3,
        out_specs=spec(VMEM),
        scratch_shapes=[
            field, field, field,
            VMEM((OWN, 2, OWN, LANES), jnp.float32),
            field,
            *(VMEM((EXT - 8 * s, 2, WIDE, LANES), jnp.float32) for s in range(1, 5)),
            VMEM(plane_shape, jnp.float32),
            VMEM((ITERS, 1024, LANES), jnp.float32),
            pltpu.SemaphoreType.DMA((4,)),
        ],
        compiler_params=params(60),
        cost_estimate=cost(200_000_000, 30_000_000),
    )(
        base, source_cells.reshape(-1), wavelet.reshape(-1), own_list, counts,
        observed.reshape(-1), z_matrix(), y_matrix(80, 96), y_matrix(64, 80), y_matrix(48, 64),
        forward_now, forward_before, adjoint_now, adjoint_after,
        x_low, x_high, y_low, y_high, c_low, c_high, planes,
    )

    parts = lax.all_to_all(parts.reshape(128, 8, LANES), everywhere, 0, 0, tiled=True)
    grid = pl.pallas_call(
        gather_kernel,
        out_shape=jax.ShapeDtypeStruct((5, 8, 160), jnp.float32),
        in_specs=[spec(SMEM), spec(VMEM)],
        out_specs=spec(VMEM),
        cost_estimate=cost(100_000, 600_000),
    )(base, parts.reshape(8, 16, 8, LANES))
    return grid.transpose(0, 2, 1)


def solution(mesh):
    return jax.shard_map(
        per_device,
        mesh=mesh,
        in_specs=(
            P("gy", None, "gx"),
            P("gx", "gy", None),
            P("gx", "gy", None),
            P("gx", "gy", None),
            P("gx", "gy", None),
            P(),
            P(),
            P(),
            P(),
        ),
        out_specs=P("gy", None, "gx"),
        check_vma=False,
    )
```
